128 devices in a mesh: role: 2 (over core), shard: 64 (over z, x, y).
Axes of the slice: x: 4, y: 4, z: 4, core: 2. Of those that a mesh axis runs over, the one named last changes fastest.
Arguments:
- emb_table: float32 [262144, 512], P(('role', 'shard')), may hold values from -3 to 3
- row_accum: float32 [262144], P(('role', 'shard')), may hold values from 1e-05 to 0.001
- owners: int32 [16384, 4, 1], P(('role', 'shard')), may hold values from 0 to 127; in each aligned block of 512 rows (0 to 511, 512 to 1023, ..., all dimensions but the last counted through in order) at most 8 rows name the same one
- local_rows: int32 [16384, 4, 4], P(('role', 'shard')), may hold values from 0 to 2047
- lengths: int32 [16384, 4], P(('role', 'shard')), may hold values from 1 to 4
- labels: int32 [16384], P(('role', 'shard')), may hold values 0 or 1
- w_hidden: bfloat16 [2048, 2048], replicated, may hold values from -0.125 to 0.125
- hidden_bias: float32 [2048], replicated, may hold values from -3 to 3
- w_logit: float32 [2048], replicated, may hold values from -0.125 to 0.125
Outputs:
- new_table: float32 [262144, 512], P(('role', 'shard'))
- w_grad: float32 [2048, 2048], P(('role', 'shard'))
The draws below stay inside these ranges and needn't reach their ends.
Inputs may be any that keep to these rules, and one draw needn't show every extreme that they name: `owners`: among the 512 bags of one device's samples, at most 8 name one owner, a bound that some block reaches.
All inputs are finite; a program needn't handle non-finite values. No bound on the sum of `labels` on one device may be relied on, other than what follows from the above.
Results may differ from the reference program's by a relative error of at most 0.00055.
The reference program's roundings to bfloat16 on the way (of `looked`, `pooled`, `dpre` and `dpooled`) count: a program that leaves them out, or rounds other values in their place, can miss the bound.
Values may be sent and summed in bfloat16 or wider, within the bound.
No kernel may reach another device: no remote copies, remote signals or barrier semaphores. Data moves between devices by JAX's collectives and lax.ppermute only.
A program may use at most 128 MiB of HBM per device.

```python
import math
import jax
import jax.numpy as jnp
import numpy as np
from jax import lax

E = 512
F = 4
H = 2048
BAG_LEN = 4
B_DEV = 128
ROWS_DEV = 2048
IN = 2048
CAP = 8
BATCH = 16384
ROWS = 262144
DEVICES = 128


def touch_ends(values, stream_key, least, high):
    longest = values.shape.index(max(values.shape))
    spots = []
    for shift in (0, 1):
        where = [jax.random.randint(jax.random.fold_in(stream_key, axis), (), 0, length) for axis, length in enumerate(values.shape)]
        where[longest] = (where[longest] + shift) % values.shape[longest]
        spots.append(tuple(where))
    return values.at[spots[0]].set(least).at[spots[1]].set(high)


def steps_of(stream_key, dims, split, smallest, top_value):
    level, own = 1.0, jax.random.fold_in(stream_key, 6)
    for axis_at, blocks in split:
        heights = jnp.exp(jax.random.uniform(jax.random.fold_in(own, axis_at), (blocks,), jnp.float32, smallest / len(split), top_value / len(split)))
        level = level * jnp.repeat(heights, dims[axis_at] // blocks).reshape([-1 if axis == axis_at else 1 for axis in range(len(dims))])
    return level


def deal_out(own_key, own, number, rows, number_of, top, bound, slope):
    order = jax.random.permutation(own_key, number_of)
    crowded, usual = portions_of(number_of, rows * top, bound, slope, True), portions_of(number_of, rows * top, bound, slope, False)
    places = jnp.arange(number_of)

    def named(sizes, rotation):
        used = int((sizes > 0).sum())
        fixed = max(1, used // 4)
        passed = fixed + (places - fixed + rotation * (used - fixed)) % max(1, number_of - fixed)
        return jnp.zeros((number_of,), jnp.int32).at[order[jnp.where(places < fixed, places, passed)]].set(jnp.asarray(sizes, jnp.int32))

    sizes = jnp.where(number % 4 == 0, named(crowded, number // 4), named(usual, number - number // 4 - 1))
    mixed = jax.random.permutation(jax.random.fold_in(own, 3), number_of)
    donor, receiver = mixed[0:number_of // 2 * 2:2], mixed[1:number_of // 2 * 2:2]
    margin = jnp.minimum(sizes[donor] - 1, bound - sizes[receiver]) // 2
    margin = jnp.where((donor == order[0]) | (receiver == order[0]) | (sizes[receiver] == 0), 0, jnp.maximum(margin, 0))
    passed = jax.random.randint(jax.random.fold_in(own, 4), (number_of // 2,), 0, 1 << 20) % (margin + 1)
    sizes = sizes.at[donor].add(-passed).at[receiver].add(passed)
    items = jnp.searchsorted(jnp.cumsum(sizes), jnp.arange(rows * top), side="right").astype(jnp.int32)
    table = items.reshape(top, rows).T
    table = table[jax.random.permutation(jax.random.fold_in(own, 1), rows)]
    rotation = jax.random.randint(jax.random.fold_in(own, 2), (rows, 1), 0, top)
    return jnp.take_along_axis(table, (jnp.arange(top)[None, :] + rotation) % top, axis=1)


def portions_of(number_of, total, reach, skew, full):
    loads = [(1 << 20) // math.isqrt(standing ** skew) + 1 for standing in range(1, number_of + 1)]
    largest = reach if full else min(reach, max(-(-total // number_of), total * loads[0] // sum(loads)))
    least = 1 if total - largest >= number_of - 1 else 0
    counts, rest = [largest] + [least] * (number_of - 1), total - largest - least * (number_of - 1)
    while rest > 0:
        candidates = [i for i in range(1, number_of) if counts[i] < largest] or [i for i in range(1, number_of) if counts[i] < reach]
        whole, left = sum([loads[i] for i in candidates]), rest
        for i in candidates:
            addition = min(reach - counts[i], max(1, left * loads[i] // whole), rest)
            counts[i] = counts[i] + addition
            rest = rest - addition
    return np.array(counts)


def gaussian(rng, dims, scale, reach, split=(), held_as=jnp.bfloat16):
    array = scale * jax.random.normal(rng, dims, jnp.float32)
    if split:
        array = array * steps_of(rng, dims, split, -0.22, 0.18)
    return jnp.clip(array, -reach, reach).astype(held_as)


def setup_inputs(seed: int = 0) -> dict:
    splits = jax.random.split(jax.random.key(seed), 10)
    emb_table = gaussian(splits[0], (ROWS, E), 0.5, 3.0, ((0, 128),), jnp.float32)
    row_accum = jnp.clip(jnp.exp(math.log(0.001) - 4.6051703 * jax.random.uniform(splits[1], (ROWS,), jnp.float32) ** steps_of(splits[1], (ROWS,), ((0, 128),), -0.2, 0.2)), 9.999999747378752e-06, 0.001)
    owners_keys = jax.random.split(jax.random.fold_in(splits[2], 1), BATCH * F // (B_DEV * F))
    owners_turns = jax.random.permutation(jax.random.fold_in(splits[2], 3), BATCH * F // (B_DEV * F))
    owners = jax.vmap(lambda own, number: deal_out(jax.random.fold_in(splits[2], 2), own, number, B_DEV * F, DEVICES, 1, CAP, 2))(owners_keys, owners_turns).reshape((BATCH, F, 1))
    local_rows = touch_ends(jax.random.randint(splits[3], (BATCH, F, BAG_LEN), 0, ROWS_DEV), jax.random.fold_in(splits[3], 1), 0, ROWS_DEV - 1).astype(jnp.int32)
    lengths = touch_ends(jax.random.randint(splits[4], (BATCH, F), 1, BAG_LEN + 1), jax.random.fold_in(splits[4], 1), 1, BAG_LEN).astype(jnp.int32)
    labels = touch_ends((jax.random.randint(splits[5], (BATCH,), 0, 4) < 1).astype(jnp.int32), jax.random.fold_in(splits[5], 1), 0, 1)
    w_hidden = gaussian(splits[6], (IN, H), IN ** -0.5, 0.125)
    hidden_bias = gaussian(splits[7], (H,), 0.5, 3.0, (), jnp.float32)
    w_logit = gaussian(splits[8], (H,), H ** -0.5, 0.125, (), jnp.float32)
    return dict(emb_table=emb_table, row_accum=row_accum, owners=owners, local_rows=local_rows, lengths=lengths, labels=labels, w_hidden=w_hidden, hidden_bias=hidden_bias, w_logit=w_logit)


learn_rate = 0.1

def reference(emb_table, row_accum, owners, local_rows, lengths, labels, w_hidden, hidden_bias, w_logit):
    ident = (owners * ROWS_DEV + local_rows).astype(jnp.int32)
    live = jnp.arange(BAG_LEN, dtype=jnp.int32)[None, None, :] < lengths[:, :, None]
    table_bf = emb_table.astype(jnp.bfloat16)
    steps = BATCH // B_DEV

    def one_block(carry, index):
        grad_sum, row_grad = carry
        start = (index * B_DEV).astype(jnp.int32)
        block_ids = lax.dynamic_slice_in_dim(ident, start, B_DEV, 0)
        block_live = lax.dynamic_slice_in_dim(live, start, B_DEV, 0)
        block_lab = lax.dynamic_slice_in_dim(labels, start, B_DEV, 0).astype(jnp.float32)
        looked = table_bf[block_ids].astype(jnp.float32)
        looked = jnp.where(block_live[..., None], looked, jnp.float32(0.0))
        pooled = lax.optimization_barrier(jnp.sum(looked, axis=2)).astype(jnp.bfloat16).reshape(B_DEV, IN)
        pre = jnp.dot(pooled, w_hidden, preferred_element_type=jnp.float32) + hidden_bias
        act = jax.nn.silu(pre)
        logit = jnp.dot(act, w_logit, precision=lax.Precision.HIGHEST)
        dlogit = jax.nn.sigmoid(logit) - block_lab
        sig = jax.nn.sigmoid(pre)
        dpre = (dlogit[:, None] * w_logit[None, :] * sig * (1.0 + pre * (1.0 - sig))).astype(jnp.bfloat16)
        dpooled = jnp.dot(dpre, w_hidden.T, preferred_element_type=jnp.float32).astype(jnp.bfloat16)
        grad_sum = grad_sum + jnp.dot(pooled.T, dpre, preferred_element_type=jnp.float32)
        bag_grad = dpooled.reshape(B_DEV, F, E).astype(jnp.float32)
        spread = jnp.where(block_live[..., None], bag_grad[:, :, None, :], jnp.float32(0.0))
        row_grad = row_grad.at[block_ids.reshape(-1)].add(spread.reshape(-1, E))
        return ((grad_sum, row_grad), None)
    start_carry = (jnp.zeros((IN, H), jnp.float32), jnp.zeros((ROWS, E), jnp.float32))
    (w_grad, row_grad), _ = lax.scan(one_block, start_carry, jnp.arange(steps, dtype=jnp.int32))
    new_accum = row_accum + lax.optimization_barrier(jnp.mean(row_grad * row_grad, axis=1))
    new_table = emb_table - learn_rate * row_grad / jnp.sqrt(new_accum + 1e-06)[:, None]
    return (new_table, w_grad)
```

```python
import jax
import jax.numpy as jnp
from jax import lax
from jax.experimental import pallas as pl
from jax.experimental.pallas import tpu as pltpu
from jax.sharding import Mesh, PartitionSpec as P

learn_rate = 0.1
AXES = ("role", "z", "x", "y")
BF = jnp.bfloat16
F32 = jnp.float32
I32 = jnp.int32


def iota(shape, dim):
    return lax.broadcasted_iota(I32, shape, dim)


def dot(a, b):
    return jnp.dot(a, b, preferred_element_type=F32)


def params(mib):
    return pltpu.CompilerParams(vmem_limit_bytes=mib << 20)


def split_int(v):
    return (v >> 6).astype(F32).astype(BF), (v & 63).astype(F32).astype(BF)


def route_kernel(own_c, own_r, rows, lens, out, tgt_c, tgt_r):
    samples, features = own_c.shape
    bag_len = rows.shape[1] // features
    devices, width = out.shape
    cap = width // bag_len
    bags = samples * features
    lane = iota((samples, devices), 1)
    sub = iota((devices, samples), 0)
    hot = jnp.concatenate(
        [(own_c[:, f : f + 1] == lane).astype(F32) for f in range(features)], axis=0
    )
    hot_t = jnp.concatenate(
        [(own_r[f : f + 1, :] == sub).astype(F32) for f in range(features)], axis=1
    )
    lower = (iota((bags, bags), 1) < iota((bags, bags), 0)).astype(F32).astype(BF)
    upper = (iota((bags, bags), 0) < iota((bags, bags), 1)).astype(F32).astype(BF)
    hot_t_bf = hot_t.astype(BF)
    rank_c = jnp.sum(dot(lower, hot.astype(BF)) * hot, axis=1, keepdims=True).astype(I32)
    rank_r = jnp.sum(dot(hot_t_bf, upper) * hot_t, axis=0, keepdims=True).astype(I32)
    column = iota((samples, width), 1)
    his, los = [], []
    for f in range(features):
        rank = rank_c[f * samples : (f + 1) * samples]
        wanted = jnp.zeros((samples, width), I32)
        for j in range(bag_len):
            k = f * bag_len + j
            live = j < lens[:, f : f + 1]
            value = jnp.where(live, rows[:, k : k + 1] + 1, 0)
            wanted = jnp.where(column == j * cap + rank, value, wanted)
        hi, lo = split_int(wanted)
        his.append(hi)
        los.append(lo)
        tgt_c[:, f : f + 1] = own_c[:, f : f + 1] * cap + rank
        tgt_r[f : f + 1, :] = (
            own_r[f : f + 1, :] * cap + rank_r[:, f * samples : (f + 1) * samples]
        )
    hi = dot(hot_t_bf, jnp.concatenate(his, axis=0)).astype(I32)
    lo = dot(hot_t_bf, jnp.concatenate(los, axis=0)).astype(I32)
    out[...] = hi * 64 + lo - 1


def route(own_c, own_r, rows, lens, devices, cap):
    samples, features = own_c.shape
    bag_len = rows.shape[1] // features
    return pl.pallas_call(
        route_kernel,
        out_shape=(
            jax.ShapeDtypeStruct((devices, bag_len * cap), I32),
            jax.ShapeDtypeStruct((samples, features), I32),
            jax.ShapeDtypeStruct((features, samples), I32),
        ),
        compiler_params=params(16),
    )(own_c, own_r, rows, lens)


def lookup_kernel(bag_len, ids, table, out):
    sources, width = ids.shape
    cap = width // bag_len
    slots = sources * cap
    depth = table.shape[0]
    hi, lo = split_int(ids[...] + 1)
    rep = (iota((slots, sources), 0) // cap == iota((slots, sources), 1)).astype(F32).astype(BF)
    mine = (iota((slots, width), 1) % cap == iota((slots, width), 0) % cap).astype(F32)
    spread = iota((width, bag_len * 128), 0) // cap == iota((width, bag_len * 128), 1) // 128
    spread = spread.astype(F32).astype(BF)
    hi = dot((dot(rep, hi) * mine).astype(BF), spread)
    lo = dot((dot(rep, lo) * mine).astype(BF), spread)
    wanted = hi * 64.0 + lo - 1.0
    lane = iota((slots, 128), 1).astype(F32)
    pieces = []
    for k in range(depth // 128):
        count = jnp.zeros((slots, 128), F32)
        for j in range(bag_len):
            count += (wanted[:, j * 128 : (j + 1) * 128] == lane + (128.0 * k)).astype(F32)
        pieces.append(count.astype(BF))
    out[...] = dot(jnp.concatenate(pieces, axis=1), table[...]).astype(BF)


def lookup(ids, table, bag_len):
    sources, width = ids.shape
    depth, wide = table.shape
    cap = width // bag_len
    block = 32
    return pl.pallas_call(
        lambda *refs: lookup_kernel(bag_len, *refs),
        grid=(sources // block,),
        in_specs=[
            pl.BlockSpec((block, width), lambda i: (i, 0)),
            pl.BlockSpec((depth, wide), lambda i: (0, 0)),
        ],
        out_specs=pl.BlockSpec((block * cap, wide), lambda i: (i, 0)),
        out_shape=jax.ShapeDtypeStruct((sources * cap, wide), BF),
        compiler_params=params(32),
        cost_estimate=pl.CostEstimate(
            flops=2 * sources * cap * depth * wide, bytes_accessed=4 << 20, transcendentals=0
        ),
    )(ids, table)


def dense_kernel(
    slots, tgt_c, tgt_r, labels, bias, head, w_hbm, pooled, dpre_out, sending, w, sems
):
    samples, features = tgt_c.shape
    total, wide = slots.shape
    copies = []
    for f in range(features):
        part = pl.ds(f * wide, wide)
        copies.append(pltpu.make_async_copy(w_hbm.at[part], w.at[part], sems.at[f]))
        copies[-1].start()
    lane = iota((samples, total), 1)
    pre = bias[...]
    for f in range(features):
        pick = (tgt_c[:, f : f + 1] == lane).astype(F32).astype(BF)
        bag = dot(pick, slots[...]).astype(BF)
        pooled[:, f * wide : (f + 1) * wide] = bag
        copies[f].wait()
        pre = pre + dot(bag, w[f * wide : (f + 1) * wide, :])
    sig = jax.nn.sigmoid(pre)
    logit = jnp.sum(pre * sig * head[...], axis=1, keepdims=True)
    dlogit = jax.nn.sigmoid(logit) - labels[...].astype(F32)
    dpre = (dlogit * head[...] * sig * (1.0 + pre * (1.0 - sig))).astype(BF)
    dpre_out[...] = dpre
    sub = iota((total, samples), 0)
    acc = jnp.zeros((total, wide), F32)
    for f in range(features):
        grad = lax.dot_general(
            dpre,
            w[f * wide : (f + 1) * wide, :],
            (((1,), (1,)), ((), ())),
            preferred_element_type=F32,
        ).astype(BF)
        put = (tgt_r[f : f + 1, :] == sub).astype(F32).astype(BF)
        acc += dot(put, grad)
    sending[...] = acc.astype(BF)


def dense(slots, tgt_c, tgt_r, labels, bias, head, w):
    samples, features = tgt_c.shape
    total, wide = slots.shape
    hidden = w.shape[1]
    vmem = pl.BlockSpec(memory_space=pltpu.VMEM)
    return pl.pallas_call(
        dense_kernel,
        in_specs=[vmem] * 6 + [pl.BlockSpec(memory_space=pl.ANY)],
        out_specs=[vmem] * 3,
        out_shape=(
            jax.ShapeDtypeStruct((samples, features * wide), BF),
            jax.ShapeDtypeStruct((samples, hidden), BF),
            jax.ShapeDtypeStruct((total, wide), BF),
        ),
        scratch_shapes=[
            pltpu.VMEM(w.shape, BF),
            pltpu.SemaphoreType.DMA((features,)),
        ],
        compiler_params=params(40),
        cost_estimate=pl.CostEstimate(
            flops=6 * samples * w.size, bytes_accessed=12 << 20, transcendentals=0
        ),
    )(slots, tgt_c, tgt_r, labels, bias, head, w)


def counts_kernel(ids, out):
    block, slots = out.shape
    bag_len = ids.shape[0]
    row = iota((block, slots), 0) + pl.program_id(0) * block
    count = jnp.zeros((block, slots), F32)
    for j in range(bag_len):
        count += (ids[j : j + 1, :] == row).astype(F32)
    out[...] = count.astype(BF)


def counts(ids, rows):
    bag_len, slots = ids.shape
    block = 256
    return pl.pallas_call(
        counts_kernel,
        grid=(rows // block,),
        in_specs=[pl.BlockSpec((bag_len, slots), lambda i: (0, 0))],
        out_specs=pl.BlockSpec((block, slots), lambda i: (i, 0)),
        out_shape=jax.ShapeDtypeStruct((rows, slots), BF),
        compiler_params=params(16),
        cost_estimate=pl.CostEstimate(
            flops=8 * rows * slots, bytes_accessed=2 * rows * slots, transcendentals=0
        ),
    )(ids)


def update_kernel(count, grads, table, accum, out):
    row_grad = dot(count[...], grads[...])
    square = jnp.sum(row_grad * row_grad, axis=1, keepdims=True)
    new_accum = accum[:, 0:1] + square * (1.0 / row_grad.shape[1])
    out[...] = table[...] - learn_rate * row_grad / jnp.sqrt(new_accum + 1e-6)


def update(count, grads, table, accum):
    rows, wide = table.shape
    slots = grads.shape[0]
    block = 256
    return pl.pallas_call(
        update_kernel,
        grid=(rows // block,),
        in_specs=[
            pl.BlockSpec((block, slots), lambda i: (i, 0)),
            pl.BlockSpec((slots, wide), lambda i: (0, 0)),
            pl.BlockSpec((block, wide), lambda i: (i, 0)),
            pl.BlockSpec((block, 128), lambda i: (i, 0)),
        ],
        out_specs=pl.BlockSpec((block, wide), lambda i: (i, 0)),
        out_shape=jax.ShapeDtypeStruct((rows, wide), F32),
        compiler_params=params(32),
        cost_estimate=pl.CostEstimate(
            flops=2 * rows * slots * wide, bytes_accessed=13 << 20, transcendentals=0
        ),
    )(count, grads, table, accum)


def per_device(
    emb_table, row_accum, owners, local_rows, lengths, labels, w_hidden, hidden_bias, w_logit
):
    devices = lax.axis_size(AXES)
    samples, features, bag_len = local_rows.shape
    rows_dev, width = emb_table.shape
    cap = 2 * samples * features // devices
    own_c = owners.reshape(samples, features)
    outgoing, tgt_c, tgt_r = route(
        own_c, own_c.T, local_rows.reshape(samples, features * bag_len), lengths, devices, cap
    )
    table_bf = emb_table.astype(BF)
    incoming = lax.all_to_all(outgoing, AXES, split_axis=0, concat_axis=0, tiled=True)
    found = lookup(incoming, table_bf, bag_len)
    slots = lax.all_to_all(
        found.reshape(devices, cap, width), AXES, split_axis=0, concat_axis=0, tiled=True
    )
    ids_r = incoming.reshape(devices, bag_len, cap).transpose(1, 0, 2).reshape(bag_len, -1)
    count = counts(ids_r, rows_dev)
    accum = jnp.broadcast_to(row_accum[:, None], (rows_dev, 128))
    pooled, dpre, sending = dense(
        slots.reshape(devices * cap, width),
        tgt_c,
        tgt_r,
        labels.reshape(samples, 1),
        hidden_bias[None, :],
        w_logit[None, :],
        w_hidden,
    )
    received = lax.all_to_all(
        sending.reshape(devices, cap, width), AXES, split_axis=0, concat_axis=0, tiled=True
    )
    w_grad = lax.dot_general(
        pooled, dpre, (((0,), (0,)), ((), ())), preferred_element_type=F32
    )
    for axis in AXES:
        w_grad = lax.psum_scatter(w_grad, axis, scatter_dimension=0, tiled=True)
    new_table = update(count, received.reshape(devices * cap, width), emb_table, accum)
    return (new_table, w_grad)


def solution(mesh):
    split = Mesh(mesh.devices.reshape(2, 4, 4, 4), AXES)
    placed = (
        P(AXES, None),
        P(AXES),
        P(AXES, None, None),
        P(AXES, None, None),
        P(AXES, None),
        P(AXES),
        P(),
        P(),
        P(),
    )
    return jax.shard_map(
        per_device,
        mesh=split,
        in_specs=placed,
        out_specs=(P(AXES, None), P(AXES, None)),
        check_vma=False,
    )
```

```python
import jax
import jax.numpy as jnp
from jax import lax
from jax.experimental import pallas as pl
from jax.experimental.pallas import tpu as pltpu
from jax.sharding import Mesh, PartitionSpec as P

learn_rate = 0.1
AXES = ("role", "z", "x", "y")
BF = jnp.bfloat16
F32 = jnp.float32
I32 = jnp.int32


def iota(shape, dim):
    return lax.broadcasted_iota(I32, shape, dim)


def dot(a, b):
    return jnp.dot(a, b, preferred_element_type=F32)


def params(mib):
    return pltpu.CompilerParams(vmem_limit_bytes=mib << 20)


def split_int(v):
    return (v >> 6).astype(F32).astype(BF), (v & 63).astype(F32).astype(BF)


def route_kernel(own_c, own_r, rows, lens, out, tgt_c, tgt_r):
    samples, features = own_c.shape
    bag_len = rows.shape[1] // features
    devices, width = out.shape
    cap = width // bag_len
    bags = samples * features
    lane = iota((samples, devices), 1)
    sub = iota((devices, samples), 0)
    hot = jnp.concatenate(
        [(own_c[:, f : f + 1] == lane).astype(F32) for f in range(features)], axis=0
    )
    hot_t = jnp.concatenate(
        [(own_r[f : f + 1, :] == sub).astype(F32) for f in range(features)], axis=1
    )
    lower = (iota((bags, bags), 1) < iota((bags, bags), 0)).astype(F32).astype(BF)
    upper = (iota((bags, bags), 0) < iota((bags, bags), 1)).astype(F32).astype(BF)
    hot_t_bf = hot_t.astype(BF)
    rank_c = jnp.sum(dot(lower, hot.astype(BF)) * hot, axis=1, keepdims=True).astype(I32)
    rank_r = jnp.sum(dot(hot_t_bf, upper) * hot_t, axis=0, keepdims=True).astype(I32)
    column = iota((samples, width), 1)
    his, los = [], []
    for f in range(features):
        rank = rank_c[f * samples : (f + 1) * samples]
        wanted = jnp.zeros((samples, width), I32)
        for j in range(bag_len):
            k = f * bag_len + j
            live = j < lens[:, f : f + 1]
            value = jnp.where(live, rows[:, k : k + 1] + 1, 0)
            wanted = jnp.where(column == j * cap + rank, value, wanted)
        hi, lo = split_int(wanted)
        his.append(hi)
        los.append(lo)
        tgt_c[:, f : f + 1] = own_c[:, f : f + 1] * cap + rank
        tgt_r[f : f + 1, :] = (
            own_r[f : f + 1, :] * cap + rank_r[:, f * samples : (f + 1) * samples]
        )
    hi = dot(hot_t_bf, jnp.concatenate(his, axis=0)).astype(I32)
    lo = dot(hot_t_bf, jnp.concatenate(los, axis=0)).astype(I32)
    out[...] = hi * 64 + lo - 1


def route(own_c, own_r, rows, lens, devices, cap):
    samples, features = own_c.shape
    bag_len = rows.shape[1] // features
    return pl.pallas_call(
        route_kernel,
        out_shape=(
            jax.ShapeDtypeStruct((devices, bag_len * cap), I32),
            jax.ShapeDtypeStruct((samples, features), I32),
            jax.ShapeDtypeStruct((features, samples), I32),
        ),
        compiler_params=params(16),
    )(own_c, own_r, rows, lens)


def lookup_kernel(bag_len, ids, table, out):
    sources, width = ids.shape
    cap = width // bag_len
    slots = sources * cap
    depth = table.shape[0]
    hi, lo = split_int(ids[...] + 1)
    rep = (iota((slots, sources), 0) // cap == iota((slots, sources), 1)).astype(F32).astype(BF)
    mine = (iota((slots, width), 1) % cap == iota((slots, width), 0) % cap).astype(F32)
    spread = iota((width, bag_len * 128), 0) // cap == iota((width, bag_len * 128), 1) // 128
    spread = spread.astype(F32).astype(BF)
    hi = dot((dot(rep, hi) * mine).astype(BF), spread)
    lo = dot((dot(rep, lo) * mine).astype(BF), spread)
    wanted = hi * 64.0 + lo - 1.0
    lane = iota((slots, 128), 1).astype(F32)
    pieces = []
    for k in range(depth // 128):
        count = jnp.zeros((slots, 128), F32)
        for j in range(bag_len):
            count += (wanted[:, j * 128 : (j + 1) * 128] == lane + (128.0 * k)).astype(F32)
        pieces.append(count.astype(BF))
    out[...] = dot(jnp.concatenate(pieces, axis=1), table[...]).astype(BF)


def lookup(ids, table, bag_len):
    sources, width = ids.shape
    depth, wide = table.shape
    cap = width // bag_len
    block = 32
    return pl.pallas_call(
        lambda *refs: lookup_kernel(bag_len, *refs),
        grid=(sources // block,),
        in_specs=[
            pl.BlockSpec((block, width), lambda i: (i, 0)),
            pl.BlockSpec((depth, wide), lambda i: (0, 0)),
        ],
        out_specs=pl.BlockSpec((block * cap, wide), lambda i: (i, 0)),
        out_shape=jax.ShapeDtypeStruct((sources * cap, wide), BF),
        compiler_params=params(32),
        cost_estimate=pl.CostEstimate(
            flops=2 * sources * cap * depth * wide, bytes_accessed=4 << 20, transcendentals=0
        ),
    )(ids, table)


def pool_kernel(slots, tgt_c, pooled, blocks):
    samples, features = tgt_c.shape
    total, wide = slots.shape
    part = blocks.shape[2]
    lane = iota((samples, total), 1)
    for f in range(features):
        pick = (tgt_c[:, f : f + 1] == lane).astype(F32).astype(BF)
        bag = dot(pick, slots[...]).astype(BF)
        pooled[:, f * wide : (f + 1) * wide] = bag
        for k in range(wide // part):
            blocks[f * (wide // part) + k] = bag[:, k * part : (k + 1) * part]


def pool(slots, tgt_c, groups):
    samples, features = tgt_c.shape
    full = features * slots.shape[1]
    return pl.pallas_call(
        pool_kernel,
        out_shape=(
            jax.ShapeDtypeStruct((samples, full), BF),
            jax.ShapeDtypeStruct((groups, samples, full // groups), BF),
        ),
        compiler_params=params(16),
    )(slots, tgt_c)


def dense_kernel(pooled, tgt_r, labels, bias, head, w_hbm, dpre_out, sending, w, sems):
    features, samples = tgt_r.shape
    total, wide = sending.shape
    copies = []
    for f in range(features):
        part = pl.ds(f * wide, wide)
        copies.append(pltpu.make_async_copy(w_hbm.at[part], w.at[part], sems.at[f]))
        copies[-1].start()
    pre = bias[...]
    for f in range(features):
        copies[f].wait()
        pre = pre + dot(pooled[:, f * wide : (f + 1) * wide], w[f * wide : (f + 1) * wide, :])
    sig = jax.nn.sigmoid(pre)
    logit = jnp.sum(pre * sig * head[...], axis=1, keepdims=True)
    dlogit = jax.nn.sigmoid(logit) - labels[...].astype(F32)
    dpre = (dlogit * head[...] * sig * (1.0 + pre * (1.0 - sig))).astype(BF)
    dpre_out[...] = dpre
    sub = iota((total, samples), 0)
    acc = jnp.zeros((total, wide), F32)
    for f in range(features):
        grad = lax.dot_general(
            dpre,
            w[f * wide : (f + 1) * wide, :],
            (((1,), (1,)), ((), ())),
            preferred_element_type=F32,
        ).astype(BF)
        put = (tgt_r[f : f + 1, :] == sub).astype(F32).astype(BF)
        acc += dot(put, grad)
    sending[...] = acc.astype(BF)


def dense(pooled, tgt_r, labels, bias, head, w, total):
    features, samples = tgt_r.shape
    hidden = w.shape[1]
    wide = w.shape[0] // features
    vmem = pl.BlockSpec(memory_space=pltpu.VMEM)
    return pl.pallas_call(
        dense_kernel,
        in_specs=[vmem] * 5 + [pl.BlockSpec(memory_space=pl.ANY)],
        out_specs=[vmem] * 2,
        out_shape=(
            jax.ShapeDtypeStruct((samples, hidden), BF),
            jax.ShapeDtypeStruct((total, wide), BF),
        ),
        scratch_shapes=[
            pltpu.VMEM(w.shape, BF),
            pltpu.SemaphoreType.DMA((features,)),
        ],
        compiler_params=params(40),
        cost_estimate=pl.CostEstimate(
            flops=6 * samples * w.size, bytes_accessed=12 << 20, transcendentals=0
        ),
    )(pooled, tgt_r, labels, bias, head, w)


def weight_kernel(order, blocks, *refs):
    pieces, out = refs[:-1], refs[-1]
    half = len(pieces) // 2
    acc = None
    for k in range(half):
        left = jnp.concatenate([blocks[order[k]], blocks[order[half + k]]], axis=0)
        right = jnp.concatenate([pieces[k][...], pieces[half + k][...]], axis=0)
        term = lax.dot_general(
            left, right, (((0,), (0,)), ((), ())), preferred_element_type=F32
        )
        acc = term if acc is None else acc + term
    out[...] = acc


def weight_part(order, blocks, pieces):
    hidden = pieces[0].shape[1]
    vmem = pl.BlockSpec(memory_space=pltpu.VMEM)
    return pl.pallas_call(
        weight_kernel,
        in_specs=[pl.BlockSpec(memory_space=pltpu.SMEM)] + [vmem] * (1 + len(pieces)),
        out_specs=vmem,
        out_shape=jax.ShapeDtypeStruct((blocks.shape[2], hidden), F32),
        compiler_params=params(32),
        cost_estimate=pl.CostEstimate(
            flops=2 * blocks.size * hidden, bytes_accessed=7 << 20, transcendentals=0
        ),
    )(order, blocks, *pieces)


def counts_kernel(ids, out):
    block, slots = out.shape
    bag_len = ids.shape[0]
    row = iota((block, slots), 0) + pl.program_id(0) * block
    count = jnp.zeros((block, slots), F32)
    for j in range(bag_len):
        count += (ids[j : j + 1, :] == row).astype(F32)
    out[...] = count.astype(BF)


def counts(ids, rows):
    bag_len, slots = ids.shape
    block = 256
    return pl.pallas_call(
        counts_kernel,
        grid=(rows // block,),
        in_specs=[pl.BlockSpec((bag_len, slots), lambda i: (0, 0))],
        out_specs=pl.BlockSpec((block, slots), lambda i: (i, 0)),
        out_shape=jax.ShapeDtypeStruct((rows, slots), BF),
        compiler_params=params(16),
        cost_estimate=pl.CostEstimate(
            flops=8 * rows * slots, bytes_accessed=2 * rows * slots, transcendentals=0
        ),
    )(ids)


def update_kernel(count, grads, table, accum, out):
    row_grad = dot(count[...], grads[...])
    square = jnp.sum(row_grad * row_grad, axis=1, keepdims=True)
    new_accum = accum[:, 0:1] + square * (1.0 / row_grad.shape[1])
    out[...] = table[...] - learn_rate * row_grad / jnp.sqrt(new_accum + 1e-6)


def update(count, grads, table, accum):
    rows, wide = table.shape
    slots = grads.shape[0]
    block = 256
    return pl.pallas_call(
        update_kernel,
        grid=(rows // block,),
        in_specs=[
            pl.BlockSpec((block, slots), lambda i: (i, 0)),
            pl.BlockSpec((slots, wide), lambda i: (0, 0)),
            pl.BlockSpec((block, wide), lambda i: (i, 0)),
            pl.BlockSpec((block, 128), lambda i: (i, 0)),
        ],
        out_specs=pl.BlockSpec((block, wide), lambda i: (i, 0)),
        out_shape=jax.ShapeDtypeStruct((rows, wide), F32),
        compiler_params=params(32),
        cost_estimate=pl.CostEstimate(
            flops=2 * rows * slots * wide, bytes_accessed=13 << 20, transcendentals=0
        ),
    )(count, grads, table, accum)


def per_device(
    emb_table, row_accum, owners, local_rows, lengths, labels, w_hidden, hidden_bias, w_logit
):
    devices = lax.axis_size(AXES)
    samples, features, bag_len = local_rows.shape
    rows_dev, width = emb_table.shape
    cap = 2 * samples * features // devices
    own_c = owners.reshape(samples, features)
    outgoing, tgt_c, tgt_r = route(
        own_c, own_c.T, local_rows.reshape(samples, features * bag_len), lengths, devices, cap
    )
    table_bf = emb_table.astype(BF)
    incoming = lax.all_to_all(outgoing, AXES, split_axis=0, concat_axis=0, tiled=True)
    found = lookup(incoming, table_bf, bag_len)
    slots = lax.all_to_all(
        found.reshape(devices, cap, width), AXES, split_axis=0, concat_axis=0, tiled=True
    )
    ids_r = incoming.reshape(devices, bag_len, cap).transpose(1, 0, 2).reshape(bag_len, -1)
    count = counts(ids_r, rows_dev)
    accum = jnp.broadcast_to(row_accum[:, None], (rows_dev, 128))
    group = lax.axis_size(("role", "z"))
    ring = lax.axis_size("z")
    pooled, blocks = pool(slots.reshape(devices * cap, width), tgt_c, group)
    blocks = lax.all_to_all(blocks, ("role", "z"), split_axis=0, concat_axis=0, tiled=True)
    dpre, sending = dense(
        pooled,
        tgt_r,
        labels.reshape(samples, 1),
        hidden_bias[None, :],
        w_logit[None, :],
        w_hidden,
        devices * cap,
    )
    mine = [dpre] + [
        lax.ppermute(dpre, "z", [(i, (i + s) % ring) for i in range(ring)]) for s in range(1, ring)
    ]
    other = [lax.ppermute(v, "role", [(0, 1), (1, 0)]) for v in mine]
    received = lax.all_to_all(
        sending.reshape(devices, cap, width), AXES, split_axis=0, concat_axis=0, tiled=True
    )
    role, z = lax.axis_index("role"), lax.axis_index("z")
    order = jnp.stack(
        [r * ring + (z - s) % ring for r in (role, 1 - role) for s in range(ring)]
    ).astype(I32)
    part = weight_part(order, blocks, mine + other)
    plane = devices // group
    part = lax.all_to_all(
        part.reshape(plane, -1, part.shape[1]), ("x", "y"), split_axis=0, concat_axis=0, tiled=True
    )
    w_grad = jnp.sum(part, axis=0)
    new_table = update(count, received.reshape(devices * cap, width), emb_table, accum)
    return (new_table, w_grad)


def solution(mesh):
    split = Mesh(mesh.devices.reshape(2, 4, 4, 4), AXES)
    placed = (
        P(AXES, None),
        P(AXES),
        P(AXES, None, None),
        P(AXES, None, None),
        P(AXES, None),
        P(AXES),
        P(),
        P(),
        P(),
    )
    return jax.shard_map(
        per_device,
        mesh=split,
        in_specs=placed,
        out_specs=(P(AXES, None), P(AXES, None)),
        check_vma=False,
    )
```

```python
import functools

import jax
import jax.numpy as jnp
from jax import lax
from jax.experimental import pallas as pl
from jax.experimental.pallas import tpu as pltpu
from jax.sharding import Mesh, PartitionSpec as P

learn_rate = 0.1
AXES = ("role", "z", "x", "y")
BF = jnp.bfloat16
F32 = jnp.float32
I32 = jnp.int32


def iota(shape, dim):
    return lax.broadcasted_iota(I32, shape, dim)


def dot(a, b):
    return jnp.dot(a, b, preferred_element_type=F32)


def dot_t(a, b):
    return lax.dot_general(a, b, (((1,), (1,)), ((), ())), preferred_element_type=F32)


def params(mib):
    return pltpu.CompilerParams(vmem_limit_bytes=mib << 20)


def cost(flops, nbytes):
    return pl.CostEstimate(flops=flops, bytes_accessed=nbytes, transcendentals=0)


SMEM = pl.BlockSpec(memory_space=pltpu.SMEM)
VMEM = pl.BlockSpec(memory_space=pltpu.VMEM)


def struct(shape, dtype):
    return jax.ShapeDtypeStruct(shape, dtype)


def split_int(v):
    return (v >> 6).astype(F32).astype(BF), (v & 63).astype(F32).astype(BF)


def route_kernel(own, rows, lens, labels, out, cols, tgt_r):
    features, bag_len, samples = rows.shape
    devices, width = out.shape
    cap = width // bag_len
    bags = samples * features
    sub = iota((devices, samples), 0)
    hot = jnp.concatenate([(own[f] == sub).astype(F32) for f in range(features)], axis=1)
    hot_bf = hot.astype(BF)
    upper = (iota((bags, bags), 0) < iota((bags, bags), 1)).astype(F32).astype(BF)
    rank = jnp.sum(dot(hot_bf, upper) * hot, axis=0, keepdims=True).astype(I32)
    column = iota((width, bags), 0)
    wanted = jnp.zeros((width, bags), I32)
    for j in range(bag_len):
        value = jnp.concatenate(
            [
                jnp.where(j < lens[f : f + 1, :], rows[f, j : j + 1, :] + 1, 0)
                for f in range(features)
            ],
            axis=1,
        )
        wanted = jnp.where(column == j * cap + rank, value, wanted)
    hi, lo = split_int(wanted)
    out[...] = dot_t(hot_bf, hi).astype(I32) * 64 + dot_t(hot_bf, lo).astype(I32) - 1
    line = iota((samples, samples), 0)
    flat = jnp.where(line == features, labels[...].astype(F32), 0.0)
    for f in range(features):
        target = own[f] * cap + rank[:, f * samples : (f + 1) * samples]
        tgt_r[f : f + 1, :] = target
        flat = jnp.where(line == f, target.astype(F32), flat)
    cols[...] = flat.T


def route(own, rows, lens, labels, devices, cap):
    features, bag_len, samples = rows.shape
    return pl.pallas_call(
        route_kernel,
        out_shape=(
            struct((devices, bag_len * cap), I32),
            struct((samples, samples), F32),
            struct((features, samples), I32),
        ),
        compiler_params=params(12),
    )(own, rows, lens, labels)


def lookup_kernel(bag_len, ids, table, out):
    sources, width = ids.shape
    cap = width // bag_len
    slots = sources * cap
    depth = table.shape[0]
    wanted = ids[...]
    hi, lo = split_int(jnp.where(wanted < 0, 4095, wanted))
    rep = (iota((slots, sources), 0) // cap == iota((slots, sources), 1)).astype(F32).astype(BF)
    mine = (iota((slots, width), 1) % cap == iota((slots, width), 0) % cap).astype(F32)
    spread = iota((width, bag_len * 128), 0) // cap == iota((width, bag_len * 128), 1) // 128
    spread = spread.astype(F32).astype(BF)
    hi = dot((dot(rep, hi) * mine).astype(BF), spread)
    lo = dot((dot(rep, lo) * mine).astype(BF), spread)
    lane = iota((slots, 128), 1)
    low, high = (lane % 64).astype(F32), (lane // 64).astype(F32)
    near = []
    for j in range(bag_len):
        part = slice(j * 128, (j + 1) * 128)
        near.append(jnp.where(lo[:, part] == low, hi[:, part] - high, -1.0).astype(BF))
    one, zero = jnp.ones((), BF), jnp.zeros((), BF)
    pieces = []
    for k in range(depth // 128):
        at = jnp.asarray(2.0 * k, BF)
        count = jnp.where(near[0] == at, one, zero)
        for j in range(1, bag_len):
            count = count + jnp.where(near[j] == at, one, zero)
        pieces.append(count)
    out[...] = dot(jnp.concatenate(pieces, axis=1), table[...]).astype(BF)


def lookup(ids, table, bag_len):
    sources, width = ids.shape
    depth, wide = table.shape
    cap = width // bag_len
    block = 32
    return pl.pallas_call(
        lambda *refs: lookup_kernel(bag_len, *refs),
        grid=(sources // block,),
        in_specs=[
            pl.BlockSpec((block, width), lambda i: (i, 0)),
            pl.BlockSpec((depth, wide), lambda i: (0, 0)),
        ],
        out_specs=pl.BlockSpec((block * cap, wide), lambda i: (i, 0)),
        out_shape=jax.ShapeDtypeStruct((sources * cap, wide), BF),
        compiler_params=params(20),
        cost_estimate=cost(2 * sources * cap * depth * wide, 4 << 20),
    )(ids, table)


def pool_kernel(at, slots, cols, pooled, *refs):
    sends, bags = refs[:-1], refs[-1]
    features, samples, wide = bags.shape
    total = slots.shape[0]
    lane = iota((samples, total), 1).astype(F32)
    for f in range(features):
        pick = (cols[:, f : f + 1] == lane).astype(F32).astype(BF)
        bag = dot(pick, slots[...]).astype(BF)
        pooled[:, f * wide : (f + 1) * wide] = bag
        bags[f] = bag
    for s, send in enumerate(sends):
        half = ((at[1] + s) % len(sends)) // 2
        for r in range(2):
            send[r] = bags[2 * r + half]


def pool(at, slots, cols, features, ring):
    samples = cols.shape[0]
    total, wide = slots.shape
    return pl.pallas_call(
        pool_kernel,
        in_specs=[SMEM, VMEM, VMEM],
        out_specs=[VMEM] * (1 + ring),
        out_shape=[struct((samples, features * wide), BF)]
        + [struct((2, samples, wide), BF)] * ring,
        scratch_shapes=[pltpu.VMEM((features, samples, wide), BF)],
        compiler_params=params(12),
        cost_estimate=cost(1 << 20, 1 << 16),
    )(at, slots, cols)


def forward_kernel(label, at, pooled, cols, bias, head, w, dpre_out, same, other):
    pre = dot(pooled[...], w[...]) + bias[...]
    sig = jax.nn.sigmoid(pre)
    logit = jnp.sum(pre * sig * head[...], axis=1, keepdims=True)
    dlogit = jax.nn.sigmoid(logit) - cols[:, label : label + 1]
    dpre = (dlogit * head[...] * sig * (1.0 + pre * (1.0 - sig))).astype(BF)
    dpre_out[...] = dpre
    half = dpre.shape[1] // 2

    @pl.when(at[1] % 2 == 0)
    def _():
        same[...] = dpre[:, :half]
        other[...] = dpre[:, half:]

    @pl.when(at[1] % 2 == 1)
    def _():
        same[...] = dpre[:, half:]
        other[...] = dpre[:, :half]


def forward(at, pooled, cols, bias, head, w, features):
    samples, hidden = pooled.shape[0], w.shape[1]
    return pl.pallas_call(
        functools.partial(forward_kernel, features),
        in_specs=[SMEM] + [VMEM] * 5,
        out_specs=[VMEM] * 3,
        out_shape=[struct((samples, hidden), BF)] + [struct((samples, hidden // 2), BF)] * 2,
        compiler_params=params(24),
        cost_estimate=cost(2 * samples * w.size, 10 << 20),
    )(at, pooled, cols, bias, head, w)


def backward_kernel(dpre, tgt_r, w, sending):
    features, samples = tgt_r.shape
    total, wide = sending.shape
    sub = iota((total, samples), 0)
    acc = jnp.zeros((total, wide), F32)
    for f in range(features):
        grad = dot_t(dpre[...], w[f * wide : (f + 1) * wide, :]).astype(BF)
        put = (tgt_r[f : f + 1, :] == sub).astype(F32).astype(BF)
        acc += dot(put, grad)
    sending[...] = acc.astype(BF)


def backward(dpre, tgt_r, w, total):
    features, samples = tgt_r.shape
    wide = w.shape[0] // features
    return pl.pallas_call(
        backward_kernel,
        in_specs=[VMEM] * 3,
        out_specs=VMEM,
        out_shape=struct((total, wide), BF),
        compiler_params=params(24),
        cost_estimate=cost(4 * samples * w.size, 10 << 20),
    )(dpre, tgt_r, w)


def turn_kernel(at, *refs):
    pieces, keep, give = refs[:-2], refs[-2], refs[-1]
    for s, piece in enumerate(pieces):
        samples = piece.shape[1]
        part = slice(s * samples, (s + 1) * samples)
        keep[:, part] = piece[at[0]].T
        give[:, part] = piece[1 - at[0]].T


def turn(at, pieces):
    _, samples, wide = pieces[0].shape
    shape = (wide, samples * len(pieces))
    return pl.pallas_call(
        turn_kernel,
        in_specs=[SMEM] + [VMEM] * len(pieces),
        out_specs=[VMEM] * 2,
        out_shape=[struct(shape, BF)] * 2,
        compiler_params=params(12),
        cost_estimate=cost(1 << 20, 2 << 20),
    )(at, *pieces)


def weight_kernel(at, keep, got, *refs):
    ring = 4
    mine, other = refs[:ring], refs[ring : 2 * ring]
    first, second = refs[2 * ring : 3 * ring], refs[3 * ring : 4 * ring]
    acc = refs[4 * ring]
    half = acc.shape[1] // 2
    left = jnp.concatenate([keep[...], got[...]], axis=1)
    right = jnp.concatenate([ref[...] for ref in mine + other], axis=0)
    acc[...] = dot(left, right)
    for s in range(ring):
        x, y = (at[2] + s) % ring, (at[3] + s) % ring
        for p in range(2):
            first[s][p * 64 : (p + 1) * 64, :] = acc[pl.ds(p * 256 + x * 64, 64), :half]
            for q in range(ring):
                k = (p * ring + q) * 16
                second[s][k : k + 16, :] = acc[pl.ds(p * 256 + q * 64 + y * 16, 16), half:]


def weight_part(at, keep, got, mine, other):
    ring = len(mine)
    wide, samples = keep.shape
    half = mine[0].shape[1]
    return pl.pallas_call(
        weight_kernel,
        in_specs=[SMEM] + [VMEM] * (2 + 2 * ring),
        out_specs=[VMEM] * (2 * ring),
        out_shape=[struct((wide // ring, half // 2), F32)] * (2 * ring),
        scratch_shapes=[pltpu.VMEM((wide, half), F32)],
        compiler_params=params(24),
        cost_estimate=cost(4 * wide * samples * half, 8 << 20),
    )(at, keep, got, *mine, *other)


def middle_kernel(at, *refs):
    ring = 4
    first, second = refs[:ring], refs[ring : 2 * ring]
    out = refs[2 * ring : 4 * ring]
    for parts, axis, outs in ((first, 3, out[:ring]), (second, 2, out[ring:])):
        acc = refs[-1]
        acc[...] = (parts[0][...] + parts[1][...]) + (parts[2][...] + parts[3][...])
        for s in range(ring):
            k = (at[axis] + s) % ring
            for p in range(2):
                outs[s][p * 16 : (p + 1) * 16, :] = acc[pl.ds(p * 64 + k * 16, 16), :]


def middle(at, first, second):
    ring = len(first)
    rows, half = first[0].shape
    return pl.pallas_call(
        middle_kernel,
        in_specs=[SMEM] + [VMEM] * (2 * ring),
        out_specs=[VMEM] * (2 * ring),
        out_shape=[struct((rows // ring, half), F32)] * (2 * ring),
        scratch_shapes=[pltpu.VMEM((rows, half), F32)],
        compiler_params=params(12),
        cost_estimate=cost(1 << 20, 3 << 20),
    )(at, *first, *second)


def last_kernel(at, *refs):
    ring = 4
    keep, give = refs[-2], refs[-1]
    half = keep.shape[1] // 2
    for k, parts in enumerate((refs[:ring], refs[ring : 2 * ring])):
        acc = (parts[0][...] + parts[1][...]) + (parts[2][...] + parts[3][...])
        even = (at[1] % 2) == 0
        keep[:, k * half : (k + 1) * half] = jnp.where(even, acc[:16], acc[16:])
        give[:, k * half : (k + 1) * half] = jnp.where(even, acc[16:], acc[:16])


def last(at, first, second):
    ring = len(first)
    rows, half = first[0].shape
    return pl.pallas_call(
        last_kernel,
        in_specs=[SMEM] + [VMEM] * (2 * ring),
        out_specs=[VMEM] * 2,
        out_shape=[struct((rows // 2, 2 * half), F32)] * 2,
        compiler_params=params(12),
        cost_estimate=cost(1 << 16, 1 << 18),
    )(at, *first, *second)


def shifted(value, axis, shift):
    ring = lax.axis_size(axis)
    return lax.ppermute(value, axis, [(i, (i + shift) % ring) for i in range(ring)])


def swapped(value):
    return lax.ppermute(value, "role", [(0, 1), (1, 0)])


def counts_kernel(ids, out):
    block, slots = out.shape
    bag_len = ids.shape[0]
    row = iota((block, slots), 0) + pl.program_id(0) * block
    count = jnp.zeros((block, slots), F32)
    for j in range(bag_len):
        count += (ids[j : j + 1, :] == row).astype(F32)
    out[...] = count.astype(BF)


def counts(ids, rows):
    bag_len, slots = ids.shape
    block = 256
    return pl.pallas_call(
        counts_kernel,
        grid=(rows // block,),
        in_specs=[pl.BlockSpec((bag_len, slots), lambda i: (0, 0))],
        out_specs=pl.BlockSpec((block, slots), lambda i: (i, 0)),
        out_shape=jax.ShapeDtypeStruct((rows, slots), BF),
        compiler_params=params(16),
        cost_estimate=pl.CostEstimate(
            flops=8 * rows * slots, bytes_accessed=2 * rows * slots, transcendentals=0
        ),
    )(ids)


def update_kernel(count, grads, table, accum, out):
    row_grad = dot(count[...], grads[...])
    square = jnp.sum(row_grad * row_grad, axis=1, keepdims=True)
    new_accum = accum[:, 0:1] + square * (1.0 / row_grad.shape[1])
    out[...] = table[...] - learn_rate * row_grad / jnp.sqrt(new_accum + 1e-6)


def update(count, grads, table, accum):
    rows, wide = table.shape
    slots = grads.shape[0]
    block = 256
    return pl.pallas_call(
        update_kernel,
        grid=(rows // block,),
        in_specs=[
            pl.BlockSpec((block, slots), lambda i: (i, 0)),
            pl.BlockSpec((slots, wide), lambda i: (0, 0)),
            pl.BlockSpec((block, wide), lambda i: (i, 0)),
            pl.BlockSpec((block, 128), lambda i: (i, 0)),
        ],
        out_specs=pl.BlockSpec((block, wide), lambda i: (i, 0)),
        out_shape=jax.ShapeDtypeStruct((rows, wide), F32),
        compiler_params=params(32),
        cost_estimate=pl.CostEstimate(
            flops=2 * rows * slots * wide, bytes_accessed=13 << 20, transcendentals=0
        ),
    )(count, grads, table, accum)


def per_device(
    emb_table, row_accum, owners, local_rows, lengths, labels, w_hidden, hidden_bias, w_logit
):
    devices = lax.axis_size(AXES)
    ring = lax.axis_size("z")
    samples, features, bag_len = local_rows.shape
    rows_dev, width = emb_table.shape
    cap = 2 * samples * features // devices
    at = jnp.stack([lax.axis_index(axis) for axis in AXES]).astype(I32)
    outgoing, cols, tgt_r = route(
        owners.transpose(1, 2, 0),
        local_rows.transpose(1, 2, 0),
        lengths.T,
        labels[None, :],
        devices,
        cap,
    )
    table_bf = emb_table.astype(BF)
    incoming = lax.all_to_all(outgoing, AXES, split_axis=0, concat_axis=0, tiled=True)
    found = lookup(incoming, table_bf, bag_len)
    slots = lax.all_to_all(
        found.reshape(devices, cap, width), AXES, split_axis=0, concat_axis=0, tiled=True
    ).reshape(devices * cap, width)
    ids_r = incoming.reshape(devices, bag_len, cap).transpose(1, 0, 2).reshape(bag_len, -1)
    count = counts(ids_r, rows_dev)
    accum = jnp.broadcast_to(row_accum[:, None], (rows_dev, 128))
    pooled, *pieces = pool(at, slots, cols, features, ring)
    pieces = [pieces[0]] + [shifted(pieces[s], "z", s) for s in range(1, ring)]
    dpre, same, diff = forward(
        at, pooled, cols, hidden_bias[None, :], w_logit[None, :], w_hidden, features
    )
    mine = [same] + [shifted(same if s % 2 == 0 else diff, "z", s) for s in range(1, ring)]
    sending = backward(dpre, tgt_r, w_hidden, devices * cap)
    received = lax.all_to_all(
        sending.reshape(devices, cap, width), AXES, split_axis=0, concat_axis=0, tiled=True
    )
    keep, give = turn(at, pieces)
    got = swapped(give)
    other = [swapped(v) for v in mine]
    parts = weight_part(at, keep, got, mine, other)
    first = [parts[0]] + [shifted(parts[s], "x", s) for s in range(1, ring)]
    second = [parts[ring]] + [shifted(parts[ring + s], "y", s) for s in range(1, ring)]
    parts = middle(at, first, second)
    first = [parts[0]] + [shifted(parts[s], "y", s) for s in range(1, ring)]
    second = [parts[ring]] + [shifted(parts[ring + s], "x", s) for s in range(1, ring)]
    mine, give = last(at, first, second)
    got = lax.ppermute(give, "z", [(i, i ^ 1) for i in range(ring)])
    even = at[1] % 2 == 0
    w_grad = jnp.concatenate(
        [jnp.where(even, mine, got), jnp.where(even, got, mine)], axis=1
    )
    new_table = update(count, received.reshape(devices * cap, width), emb_table, accum)
    return (new_table, w_grad)


def solution(mesh):
    split = Mesh(mesh.devices.reshape(2, 4, 4, 4), AXES)
    placed = (
        P(AXES, None),
        P(AXES),
        P(AXES, None, None),
        P(AXES, None, None),
        P(AXES, None),
        P(AXES),
        P(),
        P(),
        P(),
    )
    return jax.shard_map(
        per_device,
        mesh=split,
        in_specs=placed,
        out_specs=(P(AXES, None), P(AXES, None)),
        check_vma=False,
    )
```

```python
import functools
import itertools

import jax
import jax.numpy as jnp
from jax import lax
from jax.experimental import pallas as pl
from jax.experimental.pallas import tpu as pltpu
from jax.sharding import Mesh, PartitionSpec as P

learn_rate = 0.1
AXES = ("role", "z", "x", "y")
BF = jnp.bfloat16
F32 = jnp.float32
I32 = jnp.int32


def iota(shape, dim):
    return lax.broadcasted_iota(I32, shape, dim)


def dot(a, b):
    return jnp.dot(a, b, preferred_element_type=F32)


def dot_t(a, b):
    return lax.dot_general(a, b, (((1,), (1,)), ((), ())), preferred_element_type=F32)


def params(mib):
    return pltpu.CompilerParams(vmem_limit_bytes=mib << 20)


def cost(flops, nbytes):
    return pl.CostEstimate(flops=flops, bytes_accessed=nbytes, transcendentals=0)


SMEM = pl.BlockSpec(memory_space=pltpu.SMEM)
VMEM = pl.BlockSpec(memory_space=pltpu.VMEM)
HBM = pl.BlockSpec(memory_space=pltpu.HBM)


def struct(shape, dtype):
    return jax.ShapeDtypeStruct(shape, dtype)


def split_int(v):
    return (v >> 6).astype(F32).astype(BF), (v & 63).astype(F32).astype(BF)


def route_kernel(*refs):
    hbm, (out, cols, tgt_r), local, sems = refs[:4], refs[4:7], refs[7:11], refs[11]
    copies = [pltpu.make_async_copy(a, b, sems.at[k]) for k, (a, b) in enumerate(zip(hbm, local))]
    for copy in copies:
        copy.start()
    for copy in copies:
        copy.wait()
    own, rows, lens, labels = local
    features, bag_len, samples = rows.shape
    devices, width = out.shape
    cap = width // bag_len
    bags = samples * features
    sub = iota((devices, samples), 0)
    hot = jnp.concatenate([(own[f] == sub).astype(F32) for f in range(features)], axis=1)
    hot_bf = hot.astype(BF)
    upper = (iota((bags, bags), 0) < iota((bags, bags), 1)).astype(F32).astype(BF)
    rank = jnp.sum(dot(hot_bf, upper) * hot, axis=0, keepdims=True).astype(I32)
    column = iota((width, bags), 0)
    wanted = jnp.zeros((width, bags), I32)
    for j in range(bag_len):
        value = jnp.concatenate(
            [
                jnp.where(j < lens[f : f + 1, :], rows[f, j : j + 1, :] + 1, 0)
                for f in range(features)
            ],
            axis=1,
        )
        wanted = jnp.where(column == j * cap + rank, value, wanted)
    hi, lo = split_int(wanted)
    out[...] = dot_t(hot_bf, hi).astype(I32) * 64 + dot_t(hot_bf, lo).astype(I32) - 1
    line = iota((samples, samples), 0)
    flat = jnp.where(line == features, labels[...].astype(F32), 0.0)
    for f in range(features):
        target = own[f] * cap + rank[:, f * samples : (f + 1) * samples]
        tgt_r[f : f + 1, :] = target
        flat = jnp.where(line == f, target.astype(F32), flat)
    cols[...] = flat.T


def route(own, rows, lens, labels, devices, cap):
    features, bag_len, samples = rows.shape
    return pl.pallas_call(
        route_kernel,
        in_specs=[HBM] * 4,
        out_shape=(
            struct((devices, bag_len * cap), I32),
            struct((samples, samples), F32),
            struct((features, samples), I32),
        ),
        scratch_shapes=[pltpu.VMEM(v.shape, v.dtype) for v in (own, rows, lens, labels)]
        + [pltpu.SemaphoreType.DMA((4,))],
        compiler_params=params(58),
    )(own, rows, lens, labels)


def lookup_kernel(bag_len, block, ids, table, out):
    sources, width = ids.shape
    cap = width // bag_len
    slots = block * cap
    depth = table.shape[0]
    rep = (iota((slots, block), 0) // cap == iota((slots, block), 1)).astype(F32).astype(BF)
    mine = (iota((slots, width), 1) % cap == iota((slots, width), 0) % cap).astype(F32)
    spread = iota((width, bag_len * 128), 0) // cap == iota((width, bag_len * 128), 1) // 128
    spread = spread.astype(F32).astype(BF)
    lane = iota((slots, 128), 1)
    low, high = (lane % 64).astype(F32), (lane // 64).astype(F32)
    one, zero = jnp.ones((), BF), jnp.zeros((), BF)

    for i in range(sources // block):
        wanted = ids[i * block : (i + 1) * block, :]
        hi, lo = split_int(jnp.where(wanted < 0, 4095, wanted))
        hi = dot((dot(rep, hi) * mine).astype(BF), spread)
        lo = dot((dot(rep, lo) * mine).astype(BF), spread)
        near = []
        for j in range(bag_len):
            part = slice(j * 128, (j + 1) * 128)
            near.append(jnp.where(lo[:, part] == low, hi[:, part] - high, -1.0).astype(BF))
        pieces = []
        for k in range(depth // 128):
            at = jnp.asarray(2.0 * k, BF)
            count = jnp.where(near[0] == at, one, zero)
            for j in range(1, bag_len):
                count = count + jnp.where(near[j] == at, one, zero)
            pieces.append(count)
        total = dot(jnp.concatenate(pieces, axis=1), table[...])
        out[i * slots : (i + 1) * slots, :] = total.astype(BF)


def lookup(ids, table, bag_len):
    sources, width = ids.shape
    depth, wide = table.shape
    cap = width // bag_len
    return pl.pallas_call(
        functools.partial(lookup_kernel, bag_len, 32),
        in_specs=[VMEM, VMEM],
        out_specs=VMEM,
        out_shape=struct((sources * cap, wide), BF),
        compiler_params=params(24),
        cost_estimate=cost(2 * sources * cap * depth * wide, 4 << 20),
    )(ids, table)


def forward_kernel(features, at, slots, cols, bias, head, w, early, *refs):
    own, give, dpre_out, bags, blocks, quarters = refs
    total, wide = slots.shape
    samples, hidden = dpre_out.shape
    lane = iota((samples, total), 1).astype(F32)
    for f in range(features):
        pick = (cols[:, f : f + 1] == lane).astype(F32).astype(BF)
        bags[f] = dot(pick, slots[...]).astype(BF)
    for k in range(2):
        blocks[k] = bags[k]
        for z in range(4):
            start = (z % 2) * 256 + k * 128
            blocks[2 + k, :, z * 128 : (z + 1) * 128] = bags[2 + z // 2, :, start : start + 128]
    pre = bias[...]
    for f in range(features):
        pre = pre + dot(bags[f], w[f * wide : (f + 1) * wide, :])
    sig = jax.nn.sigmoid(pre)
    logit = jnp.sum(pre * sig * head[...], axis=1, keepdims=True)
    dlogit = jax.nn.sigmoid(logit) - cols[:, features : features + 1]
    dpre = (dlogit * head[...] * sig * (1.0 + pre * (1.0 - sig))).astype(BF)
    dpre_out[...] = dpre
    for q in range(4):
        quarters[q] = dpre[:, q * wide : (q + 1) * wide]
    for packs, role, ring in ((own, at[0], at[1]), (give, 1 - at[0], at[2])):
        for s in range(4):
            to = (ring + s) % 4
            packs[s, 0] = blocks[2 * role + to // 2]
            packs[s, 1] = quarters[2 * (to % 2)]
            packs[s, 2] = quarters[2 * (to % 2) + 1]


def forward(at, slots, cols, bias, head, w, features, early):
    samples, hidden = cols.shape[0], w.shape[1]
    wide = slots.shape[1]
    return pl.pallas_call(
        functools.partial(forward_kernel, features),
        in_specs=[SMEM] + [VMEM] * 5 + [HBM],
        out_specs=[VMEM] * 3,
        out_shape=[struct((4, 3, samples, wide), BF)] * 2 + [struct((samples, hidden), BF)],
        scratch_shapes=[pltpu.VMEM((4, samples, wide), BF)] * 3,
        compiler_params=params(20),
        cost_estimate=cost(2 * samples * w.size, 10 << 20),
    )(at, slots, cols, bias, head, w, early)


def merge_kernel(own, got, *outs):
    for s, out in enumerate(outs):
        out[0] = own[s]
        out[1] = got[s]


def merge(own, got):
    ring, *rest = own.shape
    return pl.pallas_call(
        merge_kernel,
        in_specs=[VMEM] * 2,
        out_specs=[VMEM] * ring,
        out_shape=[struct((2, *rest), BF)] * ring,
        compiler_params=params(16),
        cost_estimate=cost(1 << 20, 6 << 20),
    )(own, got)


def backward_kernel(dpre, tgt_r, w, sending):
    features, samples = tgt_r.shape
    total, wide = sending.shape
    sub = iota((total, samples), 0)
    acc = jnp.zeros((total, wide), F32)
    for f in range(features):
        grad = dot_t(dpre[...], w[f * wide : (f + 1) * wide, :]).astype(BF)
        put = (tgt_r[f : f + 1, :] == sub).astype(F32).astype(BF)
        acc += dot(put, grad)
    sending[...] = acc.astype(BF)


def backward(dpre, tgt_r, w, total):
    features, samples = tgt_r.shape
    wide = w.shape[0] // features
    return pl.pallas_call(
        backward_kernel,
        in_specs=[VMEM] * 3,
        out_specs=VMEM,
        out_shape=struct((total, wide), BF),
        compiler_params=params(24),
        cost_estimate=cost(8 * samples * w.size, 10 << 20),
    )(dpre, tgt_r, w)


def weight_kernel(at, *refs):
    packs, outs, acc = refs[:4], refs[4:8], refs[8]
    half = acc.shape[1] // 2
    left = jnp.concatenate([pack[k, 0] for pack in packs for k in range(2)], axis=0)
    for q in range(2):
        right = jnp.concatenate([pack[k, 1 + q] for pack in packs for k in range(2)], axis=0)
        acc[:, q * half : (q + 1) * half] = lax.dot_general(
            left, right, (((0,), (0,)), ((), ())), preferred_element_type=F32
        )
    for s in range(4):
        first = (at[3] + s) % 4
        for p in range(2):
            for q in range(4):
                row = jnp.where(
                    at[0] == 0,
                    p * 256 + first * 64 + q * 16,
                    q * 128 + p * 64 + first * 16,
                )
                k = (p * 4 + q) * 16
                outs[s][k : k + 16, :] = acc[pl.ds(pl.multiple_of(row, 16), 16), :]


def weight_part(at, packs):
    *_, samples, wide = packs[0].shape
    return pl.pallas_call(
        weight_kernel,
        in_specs=[SMEM] + [VMEM] * 4,
        out_specs=[VMEM] * 4,
        out_shape=[struct((wide // 4, 2 * wide), F32)] * 4,
        scratch_shapes=[pltpu.VMEM((wide, 2 * wide), F32)],
        compiler_params=params(24),
        cost_estimate=cost(32 * wide * samples * wide, 8 << 20),
    )(at, *packs)


def middle_kernel(at, *refs):
    parts, outs, acc = refs[:4], refs[4:8], refs[8]
    acc[...] = (parts[0][...] + parts[1][...]) + (parts[2][...] + parts[3][...])
    for s in range(4):
        second = (at[4] + s) % 4
        for p in range(2):
            row = pl.multiple_of(p * 64 + second * 16, 16)
            outs[s][p * 16 : (p + 1) * 16, :] = acc[pl.ds(row, 16), :]


def middle(at, parts):
    rows, wide = parts[0].shape
    return pl.pallas_call(
        middle_kernel,
        in_specs=[SMEM] + [VMEM] * 4,
        out_specs=[VMEM] * 4,
        out_shape=[struct((rows // 4, wide), F32)] * 4,
        scratch_shapes=[pltpu.VMEM((rows, wide), F32)],
        compiler_params=params(12),
        cost_estimate=cost(1 << 20, 3 << 20),
    )(at, *parts)


def last_kernel(at, *refs):
    parts, keep, give = refs[:4], refs[4], refs[5]
    acc = (parts[0][...] + parts[1][...]) + (parts[2][...] + parts[3][...])
    even = at[1] % 2 == 0
    keep[...] = jnp.where(even, acc[:16], acc[16:])
    give[...] = jnp.where(even, acc[16:], acc[:16])


def last(at, parts):
    rows, wide = parts[0].shape
    return pl.pallas_call(
        last_kernel,
        in_specs=[SMEM] + [VMEM] * 4,
        out_specs=[VMEM] * 2,
        out_shape=[struct((rows // 2, wide), F32)] * 2,
        compiler_params=params(12),
        cost_estimate=cost(1 << 16, 1 << 18),
    )(at, *parts)


def device(place):
    role, z, x, y = place
    return ((role * 4 + z) * 4 + x) * 4 + y


def along(value, axes, move):
    pairs = []
    for here in itertools.product(range(2), range(4), range(4), range(4)):
        to = list(here)
        axis = axes[here[0]]
        to[axis] = move(here[axis])
        pairs.append((device(here), device(to)))
    return lax.ppermute(value, AXES, pairs)


def around(values, axes):
    return [values[0]] + [
        along(value, axes, lambda i, s=s: (i + s) % 4) for s, value in enumerate(values) if s
    ]


def near_kernel(ids, near):
    bag_len, rows, slots = near.shape
    row = iota((rows, slots), 0)
    low, high = (row % 64).astype(F32), (row // 64).astype(F32)
    wanted = ids[...]
    wanted = jnp.where(wanted < 0, 4095, wanted)
    hi, lo = (wanted >> 6).astype(F32), (wanted & 63).astype(F32)
    for j in range(bag_len):
        part = jnp.where(lo[j : j + 1] == low, hi[j : j + 1] - high, -1.0)
        near[j] = part.astype(BF)


def nearby(ids):
    bag_len, slots = ids.shape
    return pl.pallas_call(
        near_kernel,
        in_specs=[VMEM],
        out_specs=VMEM,
        out_shape=struct((bag_len, 128, slots), BF),
        compiler_params=params(12),
        cost_estimate=cost(1 << 34, 1 << 20),
    )(ids)


def update_kernel(near, grads, table, accum, out):
    block, wide = table.shape
    bag_len, _, slots = near.shape
    step = pl.program_id(0)
    one, zero = jnp.ones((), BF), jnp.zeros((), BF)
    pieces, before = [], []
    for k in range(block // 128):
        chunk = step * (block // 128) + k
        here = jnp.full((128, slots), (2 * chunk).astype(F32), F32).astype(BF)
        count = jnp.where(near[0] == here, one, zero)
        for j in range(1, bag_len):
            count = count + jnp.where(near[j] == here, one, zero)
        pieces.append(count)
        before.append(jnp.broadcast_to(accum[pl.ds(chunk, 1), :], (128, 128)).T[:, 0:1])
    row_grad = dot(jnp.concatenate(pieces, axis=0), grads[...])
    square = jnp.sum(row_grad * row_grad, axis=1, keepdims=True)
    new_accum = jnp.concatenate(before, axis=0) + square * (1.0 / wide)
    out[...] = table[...] - row_grad * (learn_rate / jnp.sqrt(new_accum + 1e-6))


def update(near, grads, table, accum):
    rows, wide = table.shape
    slots = grads.shape[0]
    block = 512
    return pl.pallas_call(
        update_kernel,
        grid=(rows // block,),
        in_specs=[
            pl.BlockSpec(near.shape, lambda i: (0, 0, 0)),
            pl.BlockSpec((slots, wide), lambda i: (0, 0)),
            pl.BlockSpec((block, wide), lambda i: (i, 0)),
            pl.BlockSpec(accum.shape, lambda i: (0, 0)),
        ],
        out_specs=pl.BlockSpec((block, wide), lambda i: (i, 0)),
        out_shape=struct((rows, wide), F32),
        compiler_params=params(58),
        cost_estimate=cost(4 * rows * slots * wide, 9 << 20),
    )(near, grads, table, accum)


def per_device(
    emb_table, row_accum, owners, local_rows, lengths, labels, w_hidden, hidden_bias, w_logit
):
    devices = lax.axis_size(AXES)
    samples, features, bag_len = local_rows.shape
    rows_dev, width = emb_table.shape
    cap = 2 * samples * features // devices
    role, z, x, y = (lax.axis_index(axis) for axis in AXES)
    odd = role == 1
    at = jnp.stack(
        [
            role,
            jnp.where(odd, x, z),
            jnp.where(odd, z, x),
            jnp.where(odd, y, x),
            jnp.where(odd, z, y),
        ]
    ).astype(I32)
    outgoing, cols, tgt_r = route(
        owners.transpose(1, 2, 0),
        local_rows.transpose(1, 2, 0),
        lengths.T,
        labels[None, :],
        devices,
        cap,
    )
    table_bf = emb_table.astype(BF)
    incoming = lax.all_to_all(outgoing, AXES, split_axis=0, concat_axis=0, tiled=True)
    found = lookup(incoming, table_bf, bag_len)
    slots = lax.all_to_all(
        found.reshape(devices, cap, width), AXES, split_axis=0, concat_axis=0, tiled=True
    ).reshape(devices * cap, width)
    ids_r = incoming.reshape(devices, bag_len, cap).transpose(1, 0, 2).reshape(bag_len, -1)
    near = nearby(ids_r)
    own, give, dpre = forward(
        at, slots, cols, hidden_bias[None, :], w_logit[None, :], w_hidden, features, near
    )
    got = lax.ppermute(give, "role", [(0, 1), (1, 0)])
    sending = backward(dpre, tgt_r, w_hidden, devices * cap)
    packs = around(merge(own, got), (1, 2))
    *parts, sending = lax.optimization_barrier((*weight_part(at, packs), sending))
    received = lax.all_to_all(
        sending.reshape(devices, cap, width), AXES, split_axis=0, concat_axis=0, tiled=True
    )
    new_table = update(
        near, received.reshape(devices * cap, width), emb_table, row_accum.reshape(-1, 128)
    )
    parts = around(parts, (2, 3))
    parts = around(middle(at, parts), (3, 1))
    *parts, new_table = lax.optimization_barrier((*parts, new_table))
    mine, give = last(at, parts)
    got = along(give, (1, 2), lambda i: i ^ 1)
    even = at[1] % 2 == 0
    w_grad = jnp.concatenate([jnp.where(even, mine, got), jnp.where(even, got, mine)], axis=1)
    return (new_table, w_grad)


def solution(mesh):
    split = Mesh(mesh.devices.reshape(2, 4, 4, 4), AXES)
    placed = (
        P(AXES, None),
        P(AXES),
        P(AXES, None, None),
        P(AXES, None, None),
        P(AXES, None),
        P(AXES),
        P(),
        P(),
        P(),
    )
    return jax.shard_map(
        per_device,
        mesh=split,
        in_specs=placed,
        out_specs=(P(AXES, None), P(AXES, None)),
        check_vma=False,
    )
```

```python
import functools
import itertools

import jax
import jax.numpy as jnp
from jax import lax
from jax.experimental import pallas as pl
from jax.experimental.pallas import tpu as pltpu
from jax.sharding import Mesh, PartitionSpec as P

learn_rate = 0.1
AXES = ("role", "z", "x", "y")
BF = jnp.bfloat16
F32 = jnp.float32
I32 = jnp.int32


def iota(shape, dim):
    return lax.broadcasted_iota(I32, shape, dim)


def dot(a, b):
    return jnp.dot(a, b, preferred_element_type=F32)


def dot_t(a, b):
    return lax.dot_general(a, b, (((1,), (1,)), ((), ())), preferred_element_type=F32)


def params(mib):
    return pltpu.CompilerParams(vmem_limit_bytes=mib << 20)


def cost(flops, nbytes):
    return pl.CostEstimate(flops=flops, bytes_accessed=nbytes, transcendentals=0)


SMEM = pl.BlockSpec(memory_space=pltpu.SMEM)
VMEM = pl.BlockSpec(memory_space=pltpu.VMEM)
HBM = pl.BlockSpec(memory_space=pltpu.HBM)


def struct(shape, dtype):
    return jax.ShapeDtypeStruct(shape, dtype)


def split_int(v):
    return (v >> 6).astype(F32).astype(BF), (v & 63).astype(F32).astype(BF)


def route_kernel(*refs):
    hbm, (out, cols, tgt_r), local, sems = refs[:4], refs[4:7], refs[7:11], refs[11]
    copies = [pltpu.make_async_copy(a, b, sems.at[k]) for k, (a, b) in enumerate(zip(hbm, local))]
    for copy in copies:
        copy.start()
    for copy in copies:
        copy.wait()
    own, rows, lens, labels = local
    features, bag_len, samples = rows.shape
    devices, width = out.shape
    cap = width // bag_len
    bags = samples * features
    sub = iota((devices, samples), 0)
    hot = jnp.concatenate([(own[f] == sub).astype(F32) for f in range(features)], axis=1)
    hot_bf = hot.astype(BF)
    upper = (iota((bags, bags), 0) < iota((bags, bags), 1)).astype(F32).astype(BF)
    rank = jnp.sum(dot(hot_bf, upper) * hot, axis=0, keepdims=True).astype(I32)
    column = iota((width, bags), 0)
    wanted = jnp.zeros((width, bags), I32)
    for j in range(bag_len):
        value = jnp.concatenate(
            [
                jnp.where(j < lens[f : f + 1, :], rows[f, j : j + 1, :] + 1, 0)
                for f in range(features)
            ],
            axis=1,
        )
        wanted = jnp.where(column == j * cap + rank, value, wanted)
    hi, lo = split_int(wanted)
    out[...] = dot_t(hot_bf, hi).astype(I32) * 64 + dot_t(hot_bf, lo).astype(I32) - 1
    line = iota((samples, samples), 0)
    flat = jnp.where(line == features, labels[...].astype(F32), 0.0)
    for f in range(features):
        target = own[f] * cap + rank[:, f * samples : (f + 1) * samples]
        tgt_r[f : f + 1, :] = target
        flat = jnp.where(line == f, target.astype(F32), flat)
    cols[...] = flat.T


def route(own, rows, lens, labels, devices, cap):
    features, bag_len, samples = rows.shape
    return pl.pallas_call(
        route_kernel,
        in_specs=[HBM] * 4,
        out_shape=(
            struct((devices, bag_len * cap), I32),
            struct((samples, samples), F32),
            struct((features, samples), I32),
        ),
        scratch_shapes=[pltpu.VMEM(v.shape, v.dtype) for v in (own, rows, lens, labels)]
        + [pltpu.SemaphoreType.DMA((4,))],
        compiler_params=params(58),
    )(own, rows, lens, labels)


def lookup_kernel(bag_len, block, ids, table, out):
    sources, width = ids.shape
    cap = width // bag_len
    slots = block * cap
    depth = table.shape[0]
    rep = (iota((slots, block), 0) // cap == iota((slots, block), 1)).astype(F32).astype(BF)
    mine = (iota((slots, width), 1) % cap == iota((slots, width), 0) % cap).astype(F32)
    spread = iota((width, bag_len * 128), 0) // cap == iota((width, bag_len * 128), 1) // 128
    spread = spread.astype(F32).astype(BF)
    lane = iota((slots, 128), 1)
    low, high = (lane % 64).astype(F32), (lane // 64).astype(F32)
    one, zero = jnp.ones((), BF), jnp.zeros((), BF)

    for i in range(sources // block):
        wanted = ids[i * block : (i + 1) * block, :]
        hi, lo = split_int(jnp.where(wanted < 0, 4095, wanted))
        hi = dot((dot(rep, hi) * mine).astype(BF), spread)
        lo = dot((dot(rep, lo) * mine).astype(BF), spread)
        near = []
        for j in range(bag_len):
            part = slice(j * 128, (j + 1) * 128)
            near.append(jnp.where(lo[:, part] == low, hi[:, part] - high, -1.0).astype(BF))
        pieces = []
        for k in range(depth // 128):
            at = jnp.asarray(2.0 * k, BF)
            count = jnp.where(near[0] == at, one, zero)
            for j in range(1, bag_len):
                count = count + jnp.where(near[j] == at, one, zero)
            pieces.append(count)
        total = dot(jnp.concatenate(pieces, axis=1), table[...])
        out[i * slots : (i + 1) * slots, :] = total.astype(BF)


def lookup(ids, table, bag_len):
    sources, width = ids.shape
    depth, wide = table.shape
    cap = width // bag_len
    return pl.pallas_call(
        functools.partial(lookup_kernel, bag_len, 32),
        in_specs=[VMEM, VMEM],
        out_specs=VMEM,
        out_shape=struct((sources * cap, wide), BF),
        compiler_params=params(24),
        cost_estimate=cost(2 * sources * cap * depth * wide, 4 << 20),
    )(ids, table)


def forward_kernel(features, at, slots, cols, bias, head, w, early, *refs):
    own, give, dpre_out, bags, blocks, quarters = refs
    total, wide = slots.shape
    samples, hidden = dpre_out.shape
    lane = iota((samples, total), 1).astype(F32)
    for f in range(features):
        pick = (cols[:, f : f + 1] == lane).astype(F32).astype(BF)
        bags[f] = dot(pick, slots[...]).astype(BF)
    for k in range(2):
        blocks[k] = bags[k]
        for z in range(4):
            start = (z % 2) * 256 + k * 128
            blocks[2 + k, :, z * 128 : (z + 1) * 128] = bags[2 + z // 2, :, start : start + 128]
    pre = bias[...]
    for f in range(features):
        pre = pre + dot(bags[f], w[f * wide : (f + 1) * wide, :])
    sig = jax.nn.sigmoid(pre)
    logit = jnp.sum(pre * sig * head[...], axis=1, keepdims=True)
    dlogit = jax.nn.sigmoid(logit) - cols[:, features : features + 1]
    dpre = (dlogit * head[...] * sig * (1.0 + pre * (1.0 - sig))).astype(BF)
    dpre_out[...] = dpre
    for q in range(4):
        quarters[q] = dpre[:, q * wide : (q + 1) * wide]
    for packs, role, ring in ((own, at[0], at[1]), (give, 1 - at[0], at[2])):
        for s in range(4):
            to = (ring + s) % 4
            packs[s, 0] = blocks[2 * role + to // 2]
            packs[s, 1] = quarters[2 * (to % 2)]
            packs[s, 2] = quarters[2 * (to % 2) + 1]


def forward(at, slots, cols, bias, head, w, features, early):
    samples, hidden = cols.shape[0], w.shape[1]
    wide = slots.shape[1]
    return pl.pallas_call(
        functools.partial(forward_kernel, features),
        in_specs=[SMEM] + [VMEM] * 5 + [HBM],
        out_specs=[VMEM] * 3,
        out_shape=[struct((4, 3, samples, wide), BF)] * 2 + [struct((samples, hidden), BF)],
        scratch_shapes=[pltpu.VMEM((4, samples, wide), BF)] * 3,
        compiler_params=params(20),
        cost_estimate=cost(2 * samples * w.size, 10 << 20),
    )(at, slots, cols, bias, head, w, early)


def merge_kernel(own, got, *outs):
    for s, out in enumerate(outs):
        out[0] = own[s]
        out[1] = got[s]


def merge(own, got):
    ring, *rest = own.shape
    return pl.pallas_call(
        merge_kernel,
        in_specs=[VMEM] * 2,
        out_specs=[VMEM] * ring,
        out_shape=[struct((2, *rest), BF)] * ring,
        compiler_params=params(16),
        cost_estimate=cost(1 << 20, 6 << 20),
    )(own, got)


def backward_kernel(dpre, tgt_r, w, sending):
    features, samples = tgt_r.shape
    total, wide = sending.shape
    sub = iota((total, samples), 0)
    acc = jnp.zeros((total, wide), F32)
    for f in range(features):
        grad = dot_t(dpre[...], w[f * wide : (f + 1) * wide, :]).astype(BF)
        put = (tgt_r[f : f + 1, :] == sub).astype(F32).astype(BF)
        acc += dot(put, grad)
    sending[...] = acc.astype(BF)


def backward(dpre, tgt_r, w, total):
    features, samples = tgt_r.shape
    wide = w.shape[0] // features
    return pl.pallas_call(
        backward_kernel,
        in_specs=[VMEM] * 3,
        out_specs=VMEM,
        out_shape=struct((total, wide), BF),
        compiler_params=params(24),
        cost_estimate=cost(28 * samples * w.size, 10 << 20),
    )(dpre, tgt_r, w)


def weight_kernel(at, *refs):
    packs, outs, acc = refs[:4], refs[4:8], refs[8]
    half = acc.shape[1] // 2
    left = jnp.concatenate([pack[k, 0] for pack in packs for k in range(2)], axis=0)
    for q in range(2):
        right = jnp.concatenate([pack[k, 1 + q] for pack in packs for k in range(2)], axis=0)
        acc[:, q * half : (q + 1) * half] = lax.dot_general(
            left, right, (((0,), (0,)), ((), ())), preferred_element_type=F32
        )
    for s in range(4):
        first = (at[3] + s) % 4
        for p in range(2):
            for q in range(4):
                row = jnp.where(
                    at[0] == 0,
                    p * 256 + first * 64 + q * 16,
                    q * 128 + p * 64 + first * 16,
                )
                k = (p * 4 + q) * 16
                outs[s][k : k + 16, :] = acc[pl.ds(pl.multiple_of(row, 16), 16), :]


def weight_part(at, packs):
    *_, samples, wide = packs[0].shape
    return pl.pallas_call(
        weight_kernel,
        in_specs=[SMEM] + [VMEM] * 4,
        out_specs=[VMEM] * 4,
        out_shape=[struct((wide // 4, 2 * wide), F32)] * 4,
        scratch_shapes=[pltpu.VMEM((wide, 2 * wide), F32)],
        compiler_params=params(24),
        cost_estimate=cost(4 * 10**10, 8 << 20),
    )(at, *packs)


def middle_kernel(at, *refs):
    parts, outs, acc = refs[:4], refs[4:8], refs[8]
    acc[...] = (parts[0][...] + parts[1][...]) + (parts[2][...] + parts[3][...])
    for s in range(4):
        second = (at[4] + s) % 4
        for p in range(2):
            row = pl.multiple_of(p * 64 + second * 16, 16)
            outs[s][p * 16 : (p + 1) * 16, :] = acc[pl.ds(row, 16), :]


def middle(at, parts):
    rows, wide = parts[0].shape
    return pl.pallas_call(
        middle_kernel,
        in_specs=[SMEM] + [VMEM] * 4,
        out_specs=[VMEM] * 4,
        out_shape=[struct((rows // 4, wide), F32)] * 4,
        scratch_shapes=[pltpu.VMEM((rows, wide), F32)],
        compiler_params=params(12),
        cost_estimate=cost(1 << 20, 3 << 20),
    )(at, *parts)


def last_kernel(at, *refs):
    parts, keep, give = refs[:4], refs[4], refs[5]
    acc = (parts[0][...] + parts[1][...]) + (parts[2][...] + parts[3][...])
    even = at[1] % 2 == 0
    keep[...] = jnp.where(even, acc[:16], acc[16:])
    give[...] = jnp.where(even, acc[16:], acc[:16])


def last(at, parts):
    rows, wide = parts[0].shape
    return pl.pallas_call(
        last_kernel,
        in_specs=[SMEM] + [VMEM] * 4,
        out_specs=[VMEM] * 2,
        out_shape=[struct((rows // 2, wide), F32)] * 2,
        compiler_params=params(12),
        cost_estimate=cost(1 << 16, 1 << 18),
    )(at, *parts)


def device(place):
    role, z, x, y = place
    return ((role * 4 + z) * 4 + x) * 4 + y


def along(value, axes, move):
    pairs = []
    for here in itertools.product(range(2), range(4), range(4), range(4)):
        to = list(here)
        axis = axes[here[0]]
        to[axis] = move(here[axis])
        pairs.append((device(here), device(to)))
    return lax.ppermute(value, AXES, pairs)


def around(values, axes):
    return [values[0]] + [
        along(value, axes, lambda i, s=s: (i + s) % 4) for s, value in enumerate(values) if s
    ]


def near_kernel(ids, near):
    bag_len, rows, slots = near.shape
    row = iota((rows, slots), 0)
    low, high = (row % 64).astype(F32), (row // 64).astype(F32)
    wanted = ids[...]
    wanted = jnp.where(wanted < 0, 4095, wanted)
    hi, lo = (wanted >> 6).astype(F32), (wanted & 63).astype(F32)
    for j in range(bag_len):
        part = jnp.where(lo[j : j + 1] == low, hi[j : j + 1] - high, -1.0)
        near[j] = part.astype(BF)


def nearby(ids):
    bag_len, slots = ids.shape
    return pl.pallas_call(
        near_kernel,
        in_specs=[VMEM],
        out_specs=VMEM,
        out_shape=struct((bag_len, 128, slots), BF),
        compiler_params=params(12),
        cost_estimate=cost(1 << 34, 1 << 20),
    )(ids)


def update_kernel(near, grads, table, accum, out):
    block, wide = table.shape
    bag_len, _, slots = near.shape
    step = pl.program_id(0)
    one, zero = jnp.ones((), BF), jnp.zeros((), BF)
    pieces, before = [], []
    for k in range(block // 128):
        chunk = step * (block // 128) + k
        here = jnp.full((128, slots), (2 * chunk).astype(F32), F32).astype(BF)
        count = jnp.where(near[0] == here, one, zero)
        for j in range(1, bag_len):
            count = count + jnp.where(near[j] == here, one, zero)
        pieces.append(count)
        before.append(jnp.broadcast_to(accum[pl.ds(chunk, 1), :], (128, 128)).T[:, 0:1])
    row_grad = dot(jnp.concatenate(pieces, axis=0), grads[...])
    square = jnp.sum(row_grad * row_grad, axis=1, keepdims=True)
    new_accum = jnp.concatenate(before, axis=0) + square * (1.0 / wide)
    out[...] = table[...] - row_grad * (learn_rate / jnp.sqrt(new_accum + 1e-6))


def update(near, grads, table, accum):
    rows, wide = table.shape
    slots = grads.shape[0]
    block = 512
    return pl.pallas_call(
        update_kernel,
        grid=(rows // block,),
        in_specs=[
            pl.BlockSpec(near.shape, lambda i: (0, 0, 0)),
            pl.BlockSpec((slots, wide), lambda i: (0, 0)),
            pl.BlockSpec((block, wide), lambda i: (i, 0)),
            pl.BlockSpec(accum.shape, lambda i: (0, 0)),
        ],
        out_specs=pl.BlockSpec((block, wide), lambda i: (i, 0)),
        out_shape=struct((rows, wide), F32),
        compiler_params=params(58),
        cost_estimate=cost(4 * rows * slots * wide, 9 << 20),
    )(near, grads, table, accum)


def per_device(
    emb_table, row_accum, owners, local_rows, lengths, labels, w_hidden, hidden_bias, w_logit
):
    devices = lax.axis_size(AXES)
    samples, features, bag_len = local_rows.shape
    rows_dev, width = emb_table.shape
    cap = 2 * samples * features // devices
    role, z, x, y = (lax.axis_index(axis) for axis in AXES)
    odd = role == 1
    at = jnp.stack(
        [
            role,
            jnp.where(odd, x, z),
            jnp.where(odd, z, x),
            jnp.where(odd, y, x),
            jnp.where(odd, z, y),
        ]
    ).astype(I32)
    outgoing, cols, tgt_r = route(
        owners.transpose(1, 2, 0),
        local_rows.transpose(1, 2, 0),
        lengths.T,
        labels[None, :],
        devices,
        cap,
    )
    table_bf = emb_table.astype(BF)
    incoming = lax.all_to_all(outgoing, AXES, split_axis=0, concat_axis=0, tiled=True)
    found = lookup(incoming, table_bf, bag_len)
    slots = lax.all_to_all(
        found.reshape(devices, cap, width), AXES, split_axis=0, concat_axis=0, tiled=True
    ).reshape(devices * cap, width)
    ids_r = incoming.reshape(devices, bag_len, cap).transpose(1, 0, 2).reshape(bag_len, -1)
    near = nearby(ids_r)
    own, give, dpre = forward(
        at, slots, cols, hidden_bias[None, :], w_logit[None, :], w_hidden, features, near
    )
    got = lax.ppermute(give, "role", [(0, 1), (1, 0)])
    sending = backward(dpre, tgt_r, w_hidden, devices * cap)
    packs = around(merge(own, got), (1, 2))
    received = lax.all_to_all(
        sending.reshape(devices, cap, width), AXES, split_axis=0, concat_axis=0, tiled=True
    )
    new_table = update(
        near, received.reshape(devices * cap, width), emb_table, row_accum.reshape(-1, 128)
    )
    parts = around(weight_part(at, packs), (2, 3))
    *parts, new_table = lax.optimization_barrier((*parts, new_table))
    parts = around(middle(at, parts), (3, 1))
    mine, give = last(at, parts)
    got = along(give, (1, 2), lambda i: i ^ 1)
    even = at[1] % 2 == 0
    w_grad = jnp.concatenate([jnp.where(even, mine, got), jnp.where(even, got, mine)], axis=1)
    return (new_table, w_grad)


def solution(mesh):
    split = Mesh(mesh.devices.reshape(2, 4, 4, 4), AXES)
    placed = (
        P(AXES, None),
        P(AXES),
        P(AXES, None, None),
        P(AXES, None, None),
        P(AXES, None),
        P(AXES),
        P(),
        P(),
        P(),
    )
    return jax.shard_map(
        per_device,
        mesh=split,
        in_specs=placed,
        out_specs=(P(AXES, None), P(AXES, None)),
        check_vma=False,
    )
```

```python
import functools
import itertools

import jax
import jax.numpy as jnp
from jax import lax
from jax.experimental import pallas as pl
from jax.experimental.pallas import tpu as pltpu
from jax.sharding import Mesh, PartitionSpec as P

learn_rate = 0.1
AXES = ("role", "z", "x", "y")
BF = jnp.bfloat16
F32 = jnp.float32
I32 = jnp.int32


def iota(shape, dim):
    return lax.broadcasted_iota(I32, shape, dim)


def dot(a, b):
    return jnp.dot(a, b, preferred_element_type=F32)


def dot_t(a, b):
    return lax.dot_general(a, b, (((1,), (1,)), ((), ())), preferred_element_type=F32)


def params(mib):
    return pltpu.CompilerParams(vmem_limit_bytes=mib << 20)


def cost(flops, nbytes):
    return pl.CostEstimate(flops=flops, bytes_accessed=nbytes, transcendentals=0)


SMEM = pl.BlockSpec(memory_space=pltpu.SMEM)
VMEM = pl.BlockSpec(memory_space=pltpu.VMEM)
HBM = pl.BlockSpec(memory_space=pltpu.HBM)
ANY = pl.BlockSpec(memory_space=pl.ANY)


def struct(shape, dtype):
    return jax.ShapeDtypeStruct(shape, dtype)


def split_int(v):
    return (v >> 6).astype(F32).astype(BF), (v & 63).astype(F32).astype(BF)


def route_kernel(*refs):
    hbm, (out, cols, tgt_r), local, sems = refs[:4], refs[4:7], refs[7:11], refs[11]
    copies = [pltpu.make_async_copy(a, b, sems.at[k]) for k, (a, b) in enumerate(zip(hbm, local))]
    for copy in copies:
        copy.start()
    for copy in copies:
        copy.wait()
    own, rows, lens, labels = local
    features, bag_len, samples = rows.shape
    devices, width = out.shape
    cap = width // bag_len
    bags = samples * features
    sub = iota((devices, samples), 0)
    hot = jnp.concatenate([(own[f] == sub).astype(F32) for f in range(features)], axis=1)
    hot_bf = hot.astype(BF)
    upper = (iota((bags, bags), 0) < iota((bags, bags), 1)).astype(F32).astype(BF)
    rank = jnp.sum(dot(hot_bf, upper) * hot, axis=0, keepdims=True).astype(I32)
    column = iota((width, bags), 0)
    wanted = jnp.zeros((width, bags), I32)
    for j in range(bag_len):
        value = jnp.concatenate(
            [
                jnp.where(j < lens[f : f + 1, :], rows[f, j : j + 1, :] + 1, 0)
                for f in range(features)
            ],
            axis=1,
        )
        wanted = jnp.where(column == j * cap + rank, value, wanted)
    hi, lo = split_int(wanted)
    out[...] = dot_t(hot_bf, hi).astype(I32) * 64 + dot_t(hot_bf, lo).astype(I32) - 1
    line = iota((samples, samples), 0)
    flat = jnp.where(line == features, labels[...].astype(F32), 0.0)
    for f in range(features):
        target = own[f] * cap + rank[:, f * samples : (f + 1) * samples]
        tgt_r[f : f + 1, :] = target
        flat = jnp.where(line == f, target.astype(F32), flat)
    cols[...] = flat.T


def route(own, rows, lens, labels, devices, cap):
    features, bag_len, samples = rows.shape
    return pl.pallas_call(
        route_kernel,
        in_specs=[HBM] * 4,
        out_shape=(
            struct((devices, bag_len * cap), I32),
            struct((samples, samples), F32),
            struct((features, samples), I32),
        ),
        scratch_shapes=[pltpu.VMEM(v.shape, v.dtype) for v in (own, rows, lens, labels)]
        + [pltpu.SemaphoreType.DMA((4,))],
        compiler_params=params(58),
    )(own, rows, lens, labels)


def lookup_kernel(bag_len, block, ids, table, out, counts):
    sources, width = ids.shape
    cap = width // bag_len
    slots = block * cap
    depth = table.shape[0]
    rep = (iota((slots, block), 0) // cap == iota((slots, block), 1)).astype(F32).astype(BF)
    mine = (iota((slots, width), 1) % cap == iota((slots, width), 0) % cap).astype(F32)
    spread = iota((width, bag_len * 128), 0) // cap == iota((width, bag_len * 128), 1) // 128
    spread = spread.astype(F32).astype(BF)
    lane = iota((slots, 128), 1)
    low, high = (lane % 64).astype(F32), (lane // 64).astype(F32)
    one, zero = jnp.ones((), BF), jnp.zeros((), BF)

    for i in range(sources // block):
        wanted = ids[i * block : (i + 1) * block, :]
        hi, lo = split_int(jnp.where(wanted < 0, 4095, wanted))
        hi = dot((dot(rep, hi) * mine).astype(BF), spread)
        lo = dot((dot(rep, lo) * mine).astype(BF), spread)
        near = []
        for j in range(bag_len):
            part = slice(j * 128, (j + 1) * 128)
            near.append(jnp.where(lo[:, part] == low, hi[:, part] - high, -1.0).astype(BF))
        for k in range(depth // 128):
            at = jnp.asarray(2.0 * k, BF)
            count = jnp.where(near[0] == at, one, zero)
            for j in range(1, bag_len):
                count = count + jnp.where(near[j] == at, one, zero)
            counts[i * slots : (i + 1) * slots, k * 128 : (k + 1) * 128] = count
    out[...] = dot(counts[...], table[...]).astype(BF)


def lookup(ids, table, bag_len):
    sources, width = ids.shape
    depth, wide = table.shape
    cap = width // bag_len
    return pl.pallas_call(
        functools.partial(lookup_kernel, bag_len, 32),
        in_specs=[VMEM, VMEM],
        out_specs=VMEM,
        out_shape=struct((sources * cap, wide), BF),
        scratch_shapes=[pltpu.VMEM((sources * cap, depth), BF)],
        compiler_params=params(24),
        cost_estimate=cost(2 * sources * cap * depth * wide, 4 << 20),
    )(ids, table)


def load(hbm, vmem, sems):
    parts = sems.shape[0]
    rows = vmem.shape[0] // parts
    copies = []
    for k in range(parts):
        part = pl.ds(k * rows, rows)
        copies.append(pltpu.make_async_copy(hbm.at[part], vmem.at[part], sems.at[k]))
        copies[-1].start()
    return copies


def forward_kernel(features, at, slots, cols, bias, head, w_any, early, *refs):
    own, give, dpre_out, bags, blocks, w, sems = refs
    total, wide = slots.shape
    samples, hidden = dpre_out.shape
    copies = load(w_any, w, sems)
    lane = iota((samples, total), 1).astype(F32)
    for f in range(features):
        pick = (cols[:, f : f + 1] == lane).astype(F32).astype(BF)
        bags[f] = dot(pick, slots[...]).astype(BF)
    for k in range(2):
        blocks[k] = bags[k]
        for z in range(4):
            start = (z % 2) * 256 + k * 128
            blocks[2 + k, :, z * 128 : (z + 1) * 128] = bags[2 + z // 2, :, start : start + 128]
    pre = bias[...]
    for f in range(features):
        for copy in copies[4 * f : 4 * f + 4]:
            copy.wait()
        pre = pre + dot(bags[f], w[f * wide : (f + 1) * wide, :])
    sig = jax.nn.sigmoid(pre)
    logit = jnp.sum(pre * sig * head[...], axis=1, keepdims=True)
    dlogit = jax.nn.sigmoid(logit) - cols[:, features : features + 1]
    dpre = (dlogit * head[...] * sig * (1.0 + pre * (1.0 - sig))).astype(BF)
    dpre_out[...] = dpre
    for out, role in ((own, at[0]), (give, 1 - at[0])):
        for k in range(2):
            out[k] = blocks[2 * role + k]
        for q in range(4):
            out[2 + q] = dpre[:, q * wide : (q + 1) * wide]


def forward(at, slots, cols, bias, head, w, features, early):
    samples, hidden = cols.shape[0], w.shape[1]
    wide = slots.shape[1]
    return pl.pallas_call(
        functools.partial(forward_kernel, features),
        in_specs=[SMEM] + [VMEM] * 4 + [ANY, HBM],
        out_specs=[VMEM] * 3,
        out_shape=[struct((6, samples, wide), BF)] * 2 + [struct((samples, hidden), BF)],
        scratch_shapes=[pltpu.VMEM((4, samples, wide), BF)] * 2
        + [pltpu.VMEM(w.shape, BF), pltpu.SemaphoreType.DMA((4 * features,))],
        compiler_params=params(48),
        cost_estimate=cost(2 * samples * w.size, 10 << 20),
    )(at, slots, cols, bias, head, w, early)


def merge_kernel(at, own, got, *packs):
    for s, pack in enumerate(packs):
        to = (at[1] + s) % 4
        for k, source in enumerate((own, got)):
            pack[k, 0] = source[to // 2]
            for q in range(2):
                pack[k, 1 + q] = source[2 + 2 * (to % 2) + q]


def merge(at, own, got):
    _, samples, wide = own.shape
    return pl.pallas_call(
        merge_kernel,
        in_specs=[SMEM] + [VMEM] * 2,
        out_specs=[VMEM] * 4,
        out_shape=[struct((2, 3, samples, wide), BF)] * 4,
        compiler_params=params(16),
        cost_estimate=cost(1 << 20, 6 << 20),
    )(at, own, got)


def backward_kernel(dpre, tgt_r, w, sending):
    features, samples = tgt_r.shape
    total, wide = sending.shape
    sub = iota((total, samples), 0)
    acc = jnp.zeros((total, wide), F32)
    for f in range(features):
        grad = dot_t(dpre[...], w[f * wide : (f + 1) * wide, :]).astype(BF)
        put = (tgt_r[f : f + 1, :] == sub).astype(F32).astype(BF)
        acc += dot(put, grad)
    sending[...] = acc.astype(BF)


def backward(dpre, tgt_r, w, total):
    features, samples = tgt_r.shape
    wide = w.shape[0] // features
    return pl.pallas_call(
        backward_kernel,
        in_specs=[VMEM] * 3,
        out_specs=VMEM,
        out_shape=struct((total, wide), BF),
        compiler_params=params(24),
        cost_estimate=cost(28 * samples * w.size, 10 << 20),
    )(dpre, tgt_r, w)


def weight_kernel(at, *refs):
    packs, outs, acc = refs[:4], refs[4:8], refs[8]
    half = acc.shape[1] // 2
    left = jnp.concatenate([pack[k, 0] for pack in packs for k in range(2)], axis=0)
    for q in range(2):
        right = jnp.concatenate([pack[k, 1 + q] for pack in packs for k in range(2)], axis=0)
        acc[:, q * half : (q + 1) * half] = lax.dot_general(
            left, right, (((0,), (0,)), ((), ())), preferred_element_type=F32
        )
    for s in range(4):
        first = (at[2] + s) % 4
        for p in range(2):
            for q in range(4):
                row = jnp.where(
                    at[0] == 0,
                    p * 256 + first * 64 + q * 16,
                    q * 128 + p * 64 + first * 16,
                )
                k = (p * 4 + q) * 16
                outs[s][k : k + 16, :] = acc[pl.ds(pl.multiple_of(row, 16), 16), :]


def weight_part(at, packs):
    *_, samples, wide = packs[0].shape
    return pl.pallas_call(
        weight_kernel,
        in_specs=[SMEM] + [VMEM] * 4,
        out_specs=[VMEM] * 4,
        out_shape=[struct((wide // 4, 2 * wide), F32)] * 4,
        scratch_shapes=[pltpu.VMEM((wide, 2 * wide), F32)],
        compiler_params=params(24),
        cost_estimate=cost(4 * 10**10, 8 << 20),
    )(at, *packs)


def middle_kernel(*refs):
    parts, out = refs[:4], refs[4]
    acc = (parts[0][...] + parts[1][...]) + (parts[2][...] + parts[3][...])
    for k in range(8):
        out[k] = acc[k * 16 : (k + 1) * 16]


def middle(parts):
    rows, wide = parts[0].shape
    return pl.pallas_call(
        middle_kernel,
        in_specs=[VMEM] * 4,
        out_specs=VMEM,
        out_shape=struct((8, rows // 8, wide), F32),
        compiler_params=params(12),
        cost_estimate=cost(1 << 20, 3 << 20),
    )(*parts)


def last_kernel(parts, out):
    wide = parts.shape[2]
    for k in range(2):
        acc = (parts[4 * k] + parts[4 * k + 1]) + (parts[4 * k + 2] + parts[4 * k + 3])
        out[:, k * wide : (k + 1) * wide] = acc


def last(parts):
    _, rows, wide = parts.shape
    return pl.pallas_call(
        last_kernel,
        in_specs=[VMEM],
        out_specs=VMEM,
        out_shape=struct((rows, 2 * wide), F32),
        compiler_params=params(12),
        cost_estimate=cost(1 << 16, 1 << 18),
    )(parts)


def device(place):
    role, z, x, y = place
    return ((role * 4 + z) * 4 + x) * 4 + y


def along(value, axes, move):
    pairs = []
    for here in itertools.product(range(2), range(4), range(4), range(4)):
        to = list(here)
        axis = axes[here[0]]
        to[axis] = move(here[axis])
        pairs.append((device(here), device(to)))
    return lax.ppermute(value, AXES, pairs)


def around(values, axes):
    return [values[0]] + [
        along(value, axes, lambda i, s=s: (i + s) % 4) for s, value in enumerate(values) if s
    ]


def eights():
    groups = []
    for half, fixed in itertools.product(range(2), range(4)):
        both = [(2 * half + p, k) for p in range(2) for k in range(4)]
        groups.append([device((0, n, fixed, k)) for n, k in both])
        groups.append([device((1, k, n, fixed)) for n, k in both])
    return groups


def near_kernel(ids, near):
    bag_len, rows, slots = near.shape
    row = iota((rows, slots), 0)
    low, high = (row % 64).astype(F32), (row // 64).astype(F32)
    wanted = ids[...]
    wanted = jnp.where(wanted < 0, 4095, wanted)
    hi, lo = (wanted >> 6).astype(F32), (wanted & 63).astype(F32)
    for j in range(bag_len):
        part = jnp.where(lo[j : j + 1] == low, hi[j : j + 1] - high, -1.0)
        near[j] = part.astype(BF)


def nearby(ids):
    bag_len, slots = ids.shape
    return pl.pallas_call(
        near_kernel,
        in_specs=[VMEM],
        out_specs=VMEM,
        out_shape=struct((bag_len, 128, slots), BF),
        compiler_params=params(12),
        cost_estimate=cost(1 << 34, 1 << 20),
    )(ids)


def update_kernel(near, grads, table, accum, out):
    block, wide = table.shape
    bag_len, _, slots = near.shape
    step = pl.program_id(0)
    one, zero = jnp.ones((), BF), jnp.zeros((), BF)
    pieces, before = [], []
    for k in range(block // 128):
        chunk = step * (block // 128) + k
        here = jnp.full((128, slots), (2 * chunk).astype(F32), F32).astype(BF)
        count = jnp.where(near[0] == here, one, zero)
        for j in range(1, bag_len):
            count = count + jnp.where(near[j] == here, one, zero)
        pieces.append(count)
        before.append(jnp.broadcast_to(accum[pl.ds(chunk, 1), :], (128, 128)).T[:, 0:1])
    row_grad = dot(jnp.concatenate(pieces, axis=0), grads[...])
    square = jnp.sum(row_grad * row_grad, axis=1, keepdims=True)
    new_accum = jnp.concatenate(before, axis=0) + square * (1.0 / wide)
    out[...] = table[...] - row_grad * (learn_rate / jnp.sqrt(new_accum + 1e-6))


def update(near, grads, table, accum):
    rows, wide = table.shape
    slots = grads.shape[0]
    block = 512
    return pl.pallas_call(
        update_kernel,
        grid=(rows // block,),
        in_specs=[
            pl.BlockSpec(near.shape, lambda i: (0, 0, 0)),
            pl.BlockSpec((slots, wide), lambda i: (0, 0)),
            pl.BlockSpec((block, wide), lambda i: (i, 0)),
            pl.BlockSpec(accum.shape, lambda i: (0, 0)),
        ],
        out_specs=pl.BlockSpec((block, wide), lambda i: (i, 0)),
        out_shape=struct((rows, wide), F32),
        compiler_params=params(58),
        cost_estimate=cost(4 * rows * slots * wide, 9 << 20),
    )(near, grads, table, accum)


def per_device(
    emb_table, row_accum, owners, local_rows, lengths, labels, w_hidden, hidden_bias, w_logit
):
    devices = lax.axis_size(AXES)
    samples, features, bag_len = local_rows.shape
    rows_dev, width = emb_table.shape
    cap = 2 * samples * features // devices
    role, z, x, y = (lax.axis_index(axis) for axis in AXES)
    odd = role == 1
    at = jnp.stack(
        [
            role,
            jnp.where(odd, x, z),
            jnp.where(odd, y, x),
        ]
    ).astype(I32)
    outgoing, cols, tgt_r = route(
        owners.transpose(1, 2, 0),
        local_rows.transpose(1, 2, 0),
        lengths.T,
        labels[None, :],
        devices,
        cap,
    )
    table_bf = emb_table.astype(BF)
    incoming = lax.all_to_all(outgoing, AXES, split_axis=0, concat_axis=0, tiled=True)
    found = lookup(incoming, table_bf, bag_len)
    slots = lax.all_to_all(
        found.reshape(devices, cap, width), AXES, split_axis=0, concat_axis=0, tiled=True
    ).reshape(devices * cap, width)
    ids_r = incoming.reshape(devices, bag_len, cap).transpose(1, 0, 2).reshape(bag_len, -1)
    near = nearby(ids_r)
    own, give, dpre = forward(
        at, slots, cols, hidden_bias[None, :], w_logit[None, :], w_hidden, features, near
    )
    got = lax.ppermute(give, "role", [(0, 1), (1, 0)])
    sending = backward(dpre, tgt_r, w_hidden, devices * cap)
    packs = around(merge(at, own, got), (1, 2))
    received = lax.all_to_all(
        sending.reshape(devices, cap, width), AXES, split_axis=0, concat_axis=0, tiled=True
    )
    new_table = update(
        near, received.reshape(devices * cap, width), emb_table, row_accum.reshape(-1, 128)
    )
    parts = around(weight_part(at, packs), (2, 3))
    *parts, new_table = lax.optimization_barrier((*parts, new_table))
    part = lax.all_to_all(
        middle(parts), AXES, split_axis=0, concat_axis=0, tiled=True, axis_index_groups=eights()
    )
    w_grad = last(part)
    return (new_table, w_grad)


def solution(mesh):
    split = Mesh(mesh.devices.reshape(2, 4, 4, 4), AXES)
    placed = (
        P(AXES, None),
        P(AXES),
        P(AXES, None, None),
        P(AXES, None, None),
        P(AXES, None),
        P(AXES),
        P(),
        P(),
        P(),
    )
    return jax.shard_map(
        per_device,
        mesh=split,
        in_specs=placed,
        out_specs=(P(AXES, None), P(AXES, None)),
        check_vma=False,
    )
```

```python
import functools
import itertools

import jax
import jax.numpy as jnp
from jax import lax
from jax.experimental import pallas as pl
from jax.experimental.pallas import tpu as pltpu
from jax.sharding import Mesh, PartitionSpec as P

learn_rate = 0.1
AXES = ("role", "z", "x", "y")
BF = jnp.bfloat16
F32 = jnp.float32
I32 = jnp.int32


def iota(shape, dim):
    return lax.broadcasted_iota(I32, shape, dim)


def dot(a, b):
    return jnp.dot(a, b, preferred_element_type=F32)


def dot_t(a, b):
    return lax.dot_general(a, b, (((1,), (1,)), ((), ())), preferred_element_type=F32)


def params(mib):
    return pltpu.CompilerParams(vmem_limit_bytes=mib << 20)


def cost(flops, nbytes):
    return pl.CostEstimate(flops=flops, bytes_accessed=nbytes, transcendentals=0)


SMEM = pl.BlockSpec(memory_space=pltpu.SMEM)
VMEM = pl.BlockSpec(memory_space=pltpu.VMEM)
HBM = pl.BlockSpec(memory_space=pltpu.HBM)
ANY = pl.BlockSpec(memory_space=pl.ANY)


def struct(shape, dtype):
    return jax.ShapeDtypeStruct(shape, dtype)


def split_int(v):
    return (v >> 6).astype(F32).astype(BF), (v & 63).astype(F32).astype(BF)


def route_kernel(*refs):
    hbm, (out, cols, tgt_r), local, sems = refs[:4], refs[4:7], refs[7:11], refs[11]
    copies = [pltpu.make_async_copy(a, b, sems.at[k]) for k, (a, b) in enumerate(zip(hbm, local))]
    for copy in copies:
        copy.start()
    for copy in copies:
        copy.wait()
    own, rows, lens, labels = local
    features, bag_len, samples = rows.shape
    devices, width = out.shape
    cap = width // bag_len
    bags = samples * features
    sub = iota((devices, samples), 0)
    hot = jnp.concatenate([(own[f] == sub).astype(F32) for f in range(features)], axis=1)
    hot_bf = hot.astype(BF)
    upper = (iota((bags, bags), 0) < iota((bags, bags), 1)).astype(F32).astype(BF)
    rank = jnp.sum(dot(hot_bf, upper) * hot, axis=0, keepdims=True).astype(I32)
    column = iota((width, bags), 0)
    wanted = jnp.zeros((width, bags), I32)
    for j in range(bag_len):
        value = jnp.concatenate(
            [
                jnp.where(j < lens[f : f + 1, :], rows[f, j : j + 1, :] + 1, 0)
                for f in range(features)
            ],
            axis=1,
        )
        wanted = jnp.where(column == j * cap + rank, value, wanted)
    hi, lo = split_int(wanted)
    out[...] = dot_t(hot_bf, hi).astype(I32) * 64 + dot_t(hot_bf, lo).astype(I32) - 1
    line = iota((samples, samples), 0)
    flat = jnp.where(line == features, labels[...].astype(F32), 0.0)
    for f in range(features):
        target = own[f] * cap + rank[:, f * samples : (f + 1) * samples]
        tgt_r[f : f + 1, :] = target
        flat = jnp.where(line == f, target.astype(F32), flat)
    cols[...] = flat.T


def route(own, rows, lens, labels, devices, cap):
    features, bag_len, samples = rows.shape
    return pl.pallas_call(
        route_kernel,
        in_specs=[HBM] * 4,
        out_shape=(
            struct((devices, bag_len * cap), I32),
            struct((samples, samples), F32),
            struct((features, samples), I32),
        ),
        scratch_shapes=[pltpu.VMEM(v.shape, v.dtype) for v in (own, rows, lens, labels)]
        + [pltpu.SemaphoreType.DMA((4,))],
        compiler_params=params(58),
    )(own, rows, lens, labels)


def lookup_kernel(bag_len, block, ids, table, out, counts):
    sources, width = ids.shape
    cap = width // bag_len
    slots = block * cap
    depth = table.shape[0]
    rep = (iota((slots, block), 0) // cap == iota((slots, block), 1)).astype(F32).astype(BF)
    mine = (iota((slots, width), 1) % cap == iota((slots, width), 0) % cap).astype(F32)
    spread = iota((width, bag_len * 128), 0) // cap == iota((width, bag_len * 128), 1) // 128
    spread = spread.astype(F32).astype(BF)
    lane = iota((slots, 128), 1)
    low, high = (lane % 64).astype(F32), (lane // 64).astype(F32)
    one, zero = jnp.ones((), BF), jnp.zeros((), BF)

    for i in range(sources // block):
        wanted = ids[i * block : (i + 1) * block, :]
        hi, lo = split_int(jnp.where(wanted < 0, 4095, wanted))
        hi = dot((dot(rep, hi) * mine).astype(BF), spread)
        lo = dot((dot(rep, lo) * mine).astype(BF), spread)
        near = []
        for j in range(bag_len):
            part = slice(j * 128, (j + 1) * 128)
            near.append(jnp.where(lo[:, part] == low, hi[:, part] - high, -1.0).astype(BF))
        for k in range(depth // 128):
            at = jnp.asarray(2.0 * k, BF)
            count = jnp.where(near[0] == at, one, zero)
            for j in range(1, bag_len):
                count = count + jnp.where(near[j] == at, one, zero)
            counts[i * slots : (i + 1) * slots, k * 128 : (k + 1) * 128] = count
    out[...] = dot(counts[...], table[...]).astype(BF)


def lookup(ids, table, bag_len):
    sources, width = ids.shape
    depth, wide = table.shape
    cap = width // bag_len
    return pl.pallas_call(
        functools.partial(lookup_kernel, bag_len, 32),
        in_specs=[VMEM, VMEM],
        out_specs=VMEM,
        out_shape=struct((sources * cap, wide), BF),
        scratch_shapes=[pltpu.VMEM((sources * cap, depth), BF)],
        compiler_params=params(24),
        cost_estimate=cost(2 * sources * cap * depth * wide, 4 << 20),
    )(ids, table)


def load(hbm, vmem, sems):
    parts = sems.shape[0]
    rows = vmem.shape[0] // parts
    copies = []
    for k in range(parts):
        part = pl.ds(k * rows, rows)
        copies.append(pltpu.make_async_copy(hbm.at[part], vmem.at[part], sems.at[k]))
        copies[-1].start()
    return copies


def forward_kernel(features, at, slots, cols, bias, head, w_any, early, *refs):
    own, give, dpre_out, bags, blocks, w, sems = refs
    total, wide = slots.shape
    samples, hidden = dpre_out.shape
    copies = load(w_any, w, sems)
    lane = iota((samples, total), 1).astype(F32)
    for f in range(features):
        pick = (cols[:, f : f + 1] == lane).astype(F32).astype(BF)
        bags[f] = dot(pick, slots[...]).astype(BF)
    for k in range(2):
        blocks[k] = bags[k]
        for z in range(4):
            start = (z % 2) * 256 + k * 128
            blocks[2 + k, :, z * 128 : (z + 1) * 128] = bags[2 + z // 2, :, start : start + 128]
    pre = bias[...]
    for f in range(features):
        for copy in copies[4 * f : 4 * f + 4]:
            copy.wait()
        pre = pre + dot(bags[f], w[f * wide : (f + 1) * wide, :])
    sig = jax.nn.sigmoid(pre)
    logit = jnp.sum(pre * sig * head[...], axis=1, keepdims=True)
    dlogit = jax.nn.sigmoid(logit) - cols[:, features : features + 1]
    dpre = (dlogit * head[...] * sig * (1.0 + pre * (1.0 - sig))).astype(BF)
    dpre_out[...] = dpre
    for out, role in ((own, at[0]), (give, 1 - at[0])):
        for k in range(2):
            out[k] = blocks[2 * role + k]
        for q in range(4):
            out[2 + q] = dpre[:, q * wide : (q + 1) * wide]


def forward(at, slots, cols, bias, head, w, features, early):
    samples, hidden = cols.shape[0], w.shape[1]
    wide = slots.shape[1]
    return pl.pallas_call(
        functools.partial(forward_kernel, features),
        in_specs=[SMEM] + [VMEM] * 4 + [ANY, HBM],
        out_specs=[VMEM] * 3,
        out_shape=[struct((6, samples, wide), BF)] * 2 + [struct((samples, hidden), BF)],
        scratch_shapes=[pltpu.VMEM((4, samples, wide), BF)] * 2
        + [pltpu.VMEM(w.shape, BF), pltpu.SemaphoreType.DMA((4 * features,))],
        compiler_params=params(48),
        cost_estimate=cost(2 * samples * w.size, 10 << 20),
    )(at, slots, cols, bias, head, w, early)


def merge_kernel(at, own, got, *packs):
    for s, pack in enumerate(packs):
        to = (at[1] + s) % 4
        for k, source in enumerate((own, got)):
            pack[k, 0] = source[to // 2]
            for q in range(2):
                pack[k, 1 + q] = source[2 + 2 * (to % 2) + q]


def merge(at, own, got):
    _, samples, wide = own.shape
    return pl.pallas_call(
        merge_kernel,
        in_specs=[SMEM] + [VMEM] * 2,
        out_specs=[VMEM] * 4,
        out_shape=[struct((2, 3, samples, wide), BF)] * 4,
        compiler_params=params(16),
        cost_estimate=cost(1 << 20, 6 << 20),
    )(at, own, got)


def backward_kernel(dpre, tgt_r, w_any, early, sending, w, sems):
    features, samples = tgt_r.shape
    copies = load(w_any, w, sems)
    total, wide = sending.shape
    sub = iota((total, samples), 0)
    acc = jnp.zeros((total, wide), F32)
    for f in range(features):
        for copy in copies[4 * f : 4 * f + 4]:
            copy.wait()
        grad = dot_t(dpre[...], w[f * wide : (f + 1) * wide, :]).astype(BF)
        put = (tgt_r[f : f + 1, :] == sub).astype(F32).astype(BF)
        acc += dot(put, grad)
    sending[...] = acc.astype(BF)


def backward(dpre, tgt_r, w, total, early):
    features, samples = tgt_r.shape
    wide = w.shape[0] // features
    return pl.pallas_call(
        backward_kernel,
        in_specs=[VMEM] * 2 + [ANY, HBM],
        out_specs=VMEM,
        out_shape=struct((total, wide), BF),
        scratch_shapes=[pltpu.VMEM(w.shape, BF), pltpu.SemaphoreType.DMA((4 * features,))],
        compiler_params=params(48),
        cost_estimate=cost(28 * samples * w.size, 10 << 20),
    )(dpre, tgt_r, w, early)


def weight_kernel(at, *refs):
    packs, outs, acc = refs[:4], refs[4:8], refs[8]
    half = acc.shape[1] // 2
    left = jnp.concatenate([pack[k, 0] for pack in packs for k in range(2)], axis=0)
    for q in range(2):
        right = jnp.concatenate([pack[k, 1 + q] for pack in packs for k in range(2)], axis=0)
        acc[:, q * half : (q + 1) * half] = lax.dot_general(
            left, right, (((0,), (0,)), ((), ())), preferred_element_type=F32
        )
    for s in range(4):
        first = (at[2] + s) % 4
        for p in range(2):
            for q in range(4):
                row = jnp.where(
                    at[0] == 0,
                    p * 256 + first * 64 + q * 16,
                    q * 128 + p * 64 + first * 16,
                )
                k = (p * 4 + q) * 16
                outs[s][k : k + 16, :] = acc[pl.ds(pl.multiple_of(row, 16), 16), :]


def weight_part(at, packs):
    *_, samples, wide = packs[0].shape
    return pl.pallas_call(
        weight_kernel,
        in_specs=[SMEM] + [VMEM] * 4,
        out_specs=[VMEM] * 4,
        out_shape=[struct((wide // 4, 2 * wide), F32)] * 4,
        scratch_shapes=[pltpu.VMEM((wide, 2 * wide), F32)],
        compiler_params=params(24),
        cost_estimate=cost(4 * 10**10, 8 << 20),
    )(at, *packs)


def middle_kernel(*refs):
    parts, out = refs[:4], refs[4]
    acc = (parts[0][...] + parts[1][...]) + (parts[2][...] + parts[3][...])
    for k in range(8):
        out[k] = acc[k * 16 : (k + 1) * 16]


def middle(parts):
    rows, wide = parts[0].shape
    return pl.pallas_call(
        middle_kernel,
        in_specs=[VMEM] * 4,
        out_specs=VMEM,
        out_shape=struct((8, rows // 8, wide), F32),
        compiler_params=params(12),
        cost_estimate=cost(1 << 20, 3 << 20),
    )(*parts)


def last_kernel(parts, out):
    wide = parts.shape[2]
    for k in range(2):
        acc = (parts[4 * k] + parts[4 * k + 1]) + (parts[4 * k + 2] + parts[4 * k + 3])
        out[:, k * wide : (k + 1) * wide] = acc


def last(parts):
    _, rows, wide = parts.shape
    return pl.pallas_call(
        last_kernel,
        in_specs=[VMEM],
        out_specs=VMEM,
        out_shape=struct((rows, 2 * wide), F32),
        compiler_params=params(12),
        cost_estimate=cost(1 << 16, 1 << 18),
    )(parts)


def device(place):
    role, z, x, y = place
    return ((role * 4 + z) * 4 + x) * 4 + y


def along(value, axes, move):
    pairs = []
    for here in itertools.product(range(2), range(4), range(4), range(4)):
        to = list(here)
        axis = axes[here[0]]
        to[axis] = move(here[axis])
        pairs.append((device(here), device(to)))
    return lax.ppermute(value, AXES, pairs)


def around(values, axes):
    return [values[0]] + [
        along(value, axes, lambda i, s=s: (i + s) % 4) for s, value in enumerate(values) if s
    ]


def eights():
    groups = []
    for half, fixed in itertools.product(range(2), range(4)):
        both = [(2 * half + p, k) for p in range(2) for k in range(4)]
        groups.append([device((0, n, fixed, k)) for n, k in both])
        groups.append([device((1, k, n, fixed)) for n, k in both])
    return groups


def near_kernel(ids, near):
    bag_len, rows, slots = near.shape
    row = iota((rows, slots), 0)
    low, high = (row % 64).astype(F32), (row // 64).astype(F32)
    wanted = ids[...]
    wanted = jnp.where(wanted < 0, 4095, wanted)
    hi, lo = (wanted >> 6).astype(F32), (wanted & 63).astype(F32)
    for j in range(bag_len):
        part = jnp.where(lo[j : j + 1] == low, hi[j : j + 1] - high, -1.0)
        near[j] = part.astype(BF)


def nearby(ids):
    bag_len, slots = ids.shape
    return pl.pallas_call(
        near_kernel,
        in_specs=[VMEM],
        out_specs=VMEM,
        out_shape=struct((bag_len, 128, slots), BF),
        compiler_params=params(12),
        cost_estimate=cost(1 << 34, 1 << 20),
    )(ids)


def counts_kernel(near, after, out):
    block, slots = out.shape
    step = pl.program_id(0)
    one, zero = jnp.ones((), BF), jnp.zeros((), BF)
    for k in range(block // 128):
        chunk = step * (block // 128) + k
        here = jnp.full((128, slots), (2 * chunk).astype(F32), F32).astype(BF)
        count = jnp.where(near[0] == here, one, zero)
        for j in range(1, near.shape[0]):
            count = count + jnp.where(near[j] == here, one, zero)
        out[k * 128 : (k + 1) * 128, :] = count


def counts(near, rows, after):
    slots = near.shape[2]
    block = 512
    return pl.pallas_call(
        counts_kernel,
        grid=(rows // block,),
        in_specs=[pl.BlockSpec(near.shape, lambda i: (0, 0, 0)), HBM],
        out_specs=pl.BlockSpec((block, slots), lambda i: (i, 0)),
        out_shape=struct((rows, slots), BF),
        compiler_params=params(16),
        cost_estimate=cost(8 * rows * slots, 5 << 20),
    )(near, after)


def update_kernel(count, grads, table, accum, out):
    block, wide = table.shape
    step = pl.program_id(0)
    before = []
    for k in range(block // 128):
        chunk = step * (block // 128) + k
        before.append(jnp.broadcast_to(accum[pl.ds(chunk, 1), :], (128, 128)).T[:, 0:1])
    row_grad = dot(count[...], grads[...])
    square = jnp.sum(row_grad * row_grad, axis=1, keepdims=True)
    new_accum = jnp.concatenate(before, axis=0) + square * (1.0 / wide)
    out[...] = table[...] - row_grad * (learn_rate / jnp.sqrt(new_accum + 1e-6))


def update(count, grads, table, accum):
    rows, wide = table.shape
    slots = grads.shape[0]
    block = 512
    return pl.pallas_call(
        update_kernel,
        grid=(rows // block,),
        in_specs=[
            pl.BlockSpec((block, slots), lambda i: (i, 0)),
            pl.BlockSpec((slots, wide), lambda i: (0, 0)),
            pl.BlockSpec((block, wide), lambda i: (i, 0)),
            pl.BlockSpec(accum.shape, lambda i: (0, 0)),
        ],
        out_specs=pl.BlockSpec((block, wide), lambda i: (i, 0)),
        out_shape=struct((rows, wide), F32),
        compiler_params=params(58),
        cost_estimate=cost(4 * rows * slots * wide, 9 << 20),
    )(count, grads, table, accum)


def per_device(
    emb_table, row_accum, owners, local_rows, lengths, labels, w_hidden, hidden_bias, w_logit
):
    devices = lax.axis_size(AXES)
    samples, features, bag_len = local_rows.shape
    rows_dev, width = emb_table.shape
    cap = 2 * samples * features // devices
    role, z, x, y = (lax.axis_index(axis) for axis in AXES)
    odd = role == 1
    at = jnp.stack(
        [
            role,
            jnp.where(odd, x, z),
            jnp.where(odd, y, x),
        ]
    ).astype(I32)
    outgoing, cols, tgt_r = route(
        owners.transpose(1, 2, 0),
        local_rows.transpose(1, 2, 0),
        lengths.T,
        labels[None, :],
        devices,
        cap,
    )
    table_bf = emb_table.astype(BF)
    incoming = lax.all_to_all(outgoing, AXES, split_axis=0, concat_axis=0, tiled=True)
    found = lookup(incoming, table_bf, bag_len)
    slots = lax.all_to_all(
        found.reshape(devices, cap, width), AXES, split_axis=0, concat_axis=0, tiled=True
    ).reshape(devices * cap, width)
    ids_r = incoming.reshape(devices, bag_len, cap).transpose(1, 0, 2).reshape(bag_len, -1)
    near = nearby(ids_r)
    own, give, dpre = forward(
        at, slots, cols, hidden_bias[None, :], w_logit[None, :], w_hidden, features, near
    )
    got = lax.ppermute(give, "role", [(0, 1), (1, 0)])
    packs = merge(at, own, got)
    count = counts(near, rows_dev, packs[0])
    packs = around(packs, (1, 2))
    sending = backward(dpre, tgt_r, w_hidden, devices * cap, count)
    received = lax.all_to_all(
        sending.reshape(devices, cap, width), AXES, split_axis=0, concat_axis=0, tiled=True
    )
    new_table = update(
        count, received.reshape(devices * cap, width), emb_table, row_accum.reshape(-1, 128)
    )
    parts = around(weight_part(at, packs), (2, 3))
    *parts, new_table = lax.optimization_barrier((*parts, new_table))
    part = lax.all_to_all(
        middle(parts), AXES, split_axis=0, concat_axis=0, tiled=True, axis_index_groups=eights()
    )
    w_grad = last(part)
    return (new_table, w_grad)


def solution(mesh):
    split = Mesh(mesh.devices.reshape(2, 4, 4, 4), AXES)
    placed = (
        P(AXES, None),
        P(AXES),
        P(AXES, None, None),
        P(AXES, None, None),
        P(AXES, None),
        P(AXES),
        P(),
        P(),
        P(),
    )
    return jax.shard_map(
        per_device,
        mesh=split,
        in_specs=placed,
        out_specs=(P(AXES, None), P(AXES, None)),
        check_vma=False,
    )
```

```python
import functools
import itertools

import jax
import jax.numpy as jnp
from jax import lax
from jax.experimental import pallas as pl
from jax.experimental.pallas import tpu as pltpu
from jax.sharding import Mesh, PartitionSpec as P

learn_rate = 0.1
AXES = ("role", "z", "x", "y")
BF = jnp.bfloat16
F32 = jnp.float32
I32 = jnp.int32


def iota(shape, dim):
    return lax.broadcasted_iota(I32, shape, dim)


def dot(a, b):
    return jnp.dot(a, b, preferred_element_type=F32)


def dot_t(a, b):
    return lax.dot_general(a, b, (((1,), (1,)), ((), ())), preferred_element_type=F32)


def params(mib):
    return pltpu.CompilerParams(vmem_limit_bytes=mib << 20)


def cost(flops, nbytes):
    return pl.CostEstimate(flops=flops, bytes_accessed=nbytes, transcendentals=0)


SMEM = pl.BlockSpec(memory_space=pltpu.SMEM)
VMEM = pl.BlockSpec(memory_space=pltpu.VMEM)
HBM = pl.BlockSpec(memory_space=pltpu.HBM)
ANY = pl.BlockSpec(memory_space=pl.ANY)


def struct(shape, dtype):
    return jax.ShapeDtypeStruct(shape, dtype)


def split_int(v):
    return (v >> 6).astype(F32).astype(BF), (v & 63).astype(F32).astype(BF)


def route_kernel(*refs):
    hbm, (out, cols, tgt_r), local, sems = refs[:4], refs[4:7], refs[7:11], refs[11]
    copies = [pltpu.make_async_copy(a, b, sems.at[k]) for k, (a, b) in enumerate(zip(hbm, local))]
    for copy in copies:
        copy.start()
    for copy in copies:
        copy.wait()
    own, rows, lens, labels = local
    features, bag_len, samples = rows.shape
    devices, width = out.shape
    cap = width // bag_len
    bags = samples * features
    sub = iota((devices, samples), 0)
    hot = jnp.concatenate([(own[f] == sub).astype(F32) for f in range(features)], axis=1)
    hot_bf = hot.astype(BF)
    upper = (iota((bags, bags), 0) < iota((bags, bags), 1)).astype(F32).astype(BF)
    rank = jnp.sum(dot(hot_bf, upper) * hot, axis=0, keepdims=True).astype(I32)
    column = iota((width, bags), 0)
    wanted = jnp.zeros((width, bags), I32)
    for j in range(bag_len):
        value = jnp.concatenate(
            [
                jnp.where(j < lens[f : f + 1, :], rows[f, j : j + 1, :] + 1, 0)
                for f in range(features)
            ],
            axis=1,
        )
        wanted = jnp.where(column == j * cap + rank, value, wanted)
    hi, lo = split_int(wanted)
    out[...] = dot_t(hot_bf, hi).astype(I32) * 64 + dot_t(hot_bf, lo).astype(I32) - 1
    line = iota((samples, samples), 0)
    flat = jnp.where(line == features, labels[...].astype(F32), 0.0)
    for f in range(features):
        target = own[f] * cap + rank[:, f * samples : (f + 1) * samples]
        tgt_r[f : f + 1, :] = target
        flat = jnp.where(line == f, target.astype(F32), flat)
    cols[...] = flat.T


def route(own, rows, lens, labels, devices, cap):
    features, bag_len, samples = rows.shape
    return pl.pallas_call(
        route_kernel,
        in_specs=[HBM] * 4,
        out_shape=(
            struct((devices, bag_len * cap), I32),
            struct((samples, samples), F32),
            struct((features, samples), I32),
        ),
        scratch_shapes=[pltpu.VMEM(v.shape, v.dtype) for v in (own, rows, lens, labels)]
        + [pltpu.SemaphoreType.DMA((4,))],
        compiler_params=params(58),
    )(own, rows, lens, labels)


def lookup_kernel(bag_len, block, ids, table, out, counts):
    sources, width = ids.shape
    cap = width // bag_len
    slots = block * cap
    depth = table.shape[0]
    rep = (iota((slots, block), 0) // cap == iota((slots, block), 1)).astype(F32).astype(BF)
    mine = (iota((slots, width), 1) % cap == iota((slots, width), 0) % cap).astype(F32)
    spread = iota((width, bag_len * 128), 0) // cap == iota((width, bag_len * 128), 1) // 128
    spread = spread.astype(F32).astype(BF)
    lane = iota((slots, 128), 1)
    low, high = (lane % 64).astype(F32), (lane // 64).astype(F32)
    one, zero = jnp.ones((), BF), jnp.zeros((), BF)

    for i in range(sources // block):
        wanted = ids[i * block : (i + 1) * block, :]
        hi, lo = split_int(jnp.where(wanted < 0, 4095, wanted))
        hi = dot((dot(rep, hi) * mine).astype(BF), spread)
        lo = dot((dot(rep, lo) * mine).astype(BF), spread)
        near = []
        for j in range(bag_len):
            part = slice(j * 128, (j + 1) * 128)
            near.append(jnp.where(lo[:, part] == low, hi[:, part] - high, -1.0).astype(BF))
        for k in range(depth // 128):
            at = jnp.asarray(2.0 * k, BF)
            count = jnp.where(near[0] == at, one, zero)
            for j in range(1, bag_len):
                count = count + jnp.where(near[j] == at, one, zero)
            counts[i * slots : (i + 1) * slots, k * 128 : (k + 1) * 128] = count
    out[...] = dot(counts[...], table[...]).astype(BF)


def lookup(ids, table, bag_len):
    sources, width = ids.shape
    depth, wide = table.shape
    cap = width // bag_len
    return pl.pallas_call(
        functools.partial(lookup_kernel, bag_len, 32),
        in_specs=[VMEM, VMEM],
        out_specs=VMEM,
        out_shape=struct((sources * cap, wide), BF),
        scratch_shapes=[pltpu.VMEM((sources * cap, depth), BF)],
        compiler_params=params(24),
        cost_estimate=cost(2 * sources * cap * depth * wide, 4 << 20),
    )(ids, table)


def load(hbm, vmem, sems):
    parts = sems.shape[0]
    rows = vmem.shape[0] // parts
    copies = []
    for k in range(parts):
        part = pl.ds(k * rows, rows)
        copies.append(pltpu.make_async_copy(hbm.at[part], vmem.at[part], sems.at[k]))
        copies[-1].start()
    return copies


def forward_kernel(features, at, slots, cols, bias, head, w_any, early, *refs):
    own, give, dpre_out, bags, blocks, w, sems = refs
    total, wide = slots.shape
    samples, hidden = dpre_out.shape
    copies = load(w_any, w, sems)
    lane = iota((samples, total), 1).astype(F32)
    for f in range(features):
        pick = (cols[:, f : f + 1] == lane).astype(F32).astype(BF)
        bags[f] = dot(pick, slots[...]).astype(BF)
    for k in range(2):
        blocks[k] = bags[k]
        for z in range(4):
            start = (z % 2) * 256 + k * 128
            blocks[2 + k, :, z * 128 : (z + 1) * 128] = bags[2 + z // 2, :, start : start + 128]
    pre = bias[...]
    for f in range(features):
        for copy in copies[4 * f : 4 * f + 4]:
            copy.wait()
        pre = pre + dot(bags[f], w[f * wide : (f + 1) * wide, :])
    sig = jax.nn.sigmoid(pre)
    logit = jnp.sum(pre * sig * head[...], axis=1, keepdims=True)
    dlogit = jax.nn.sigmoid(logit) - cols[:, features : features + 1]
    dpre = (dlogit * head[...] * sig * (1.0 + pre * (1.0 - sig))).astype(BF)
    dpre_out[...] = dpre
    for out, role in ((own, at[0]), (give, 1 - at[0])):
        for k in range(2):
            out[k] = blocks[2 * role + k]
        for q in range(4):
            out[2 + q] = dpre[:, q * wide : (q + 1) * wide]


def forward(at, slots, cols, bias, head, w, features, early):
    samples, hidden = cols.shape[0], w.shape[1]
    wide = slots.shape[1]
    return pl.pallas_call(
        functools.partial(forward_kernel, features),
        in_specs=[SMEM] + [VMEM] * 4 + [ANY, HBM],
        out_specs=[VMEM] * 3,
        out_shape=[struct((6, samples, wide), BF)] * 2 + [struct((samples, hidden), BF)],
        scratch_shapes=[pltpu.VMEM((4, samples, wide), BF)] * 2
        + [pltpu.VMEM(w.shape, BF), pltpu.SemaphoreType.DMA((4 * features,))],
        compiler_params=params(48),
        cost_estimate=cost(2 * samples * w.size, 10 << 20),
    )(at, slots, cols, bias, head, w, early)


def merge_kernel(at, own, got, *packs):
    for s, pack in enumerate(packs):
        to = (at[1] + s) % 4
        for k, source in enumerate((own, got)):
            pack[k, 0] = source[to // 2]
            for q in range(2):
                pack[k, 1 + q] = source[2 + 2 * (to % 2) + q]


def merge(at, own, got):
    _, samples, wide = own.shape
    return pl.pallas_call(
        merge_kernel,
        in_specs=[SMEM] + [VMEM] * 2,
        out_specs=[VMEM] * 4,
        out_shape=[struct((2, 3, samples, wide), BF)] * 4,
        compiler_params=params(16),
        cost_estimate=cost(1 << 20, 6 << 20),
    )(at, own, got)


def backward_kernel(dpre, tgt_r, w_any, early, sending, w, sems):
    features, samples = tgt_r.shape
    copies = load(w_any, w, sems)
    total, wide = sending.shape
    sub = iota((total, samples), 0)
    acc = jnp.zeros((total, wide), F32)
    for f in range(features):
        for copy in copies[4 * f : 4 * f + 4]:
            copy.wait()
        grad = dot_t(dpre[...], w[f * wide : (f + 1) * wide, :]).astype(BF)
        put = (tgt_r[f : f + 1, :] == sub).astype(F32).astype(BF)
        acc += dot(put, grad)
    sending[...] = acc.astype(BF)


def backward(dpre, tgt_r, w, total, early):
    features, samples = tgt_r.shape
    wide = w.shape[0] // features
    return pl.pallas_call(
        backward_kernel,
        in_specs=[VMEM] * 2 + [ANY, HBM],
        out_specs=VMEM,
        out_shape=struct((total, wide), BF),
        scratch_shapes=[pltpu.VMEM(w.shape, BF), pltpu.SemaphoreType.DMA((4 * features,))],
        compiler_params=params(48),
        cost_estimate=cost(28 * samples * w.size, 10 << 20),
    )(dpre, tgt_r, w, early)


def weight_kernel(at, *refs):
    packs, outs, acc = refs[:4], refs[4:8], refs[8]
    half = acc.shape[1] // 2
    left = jnp.concatenate([pack[k, 0] for pack in packs for k in range(2)], axis=0)
    for q in range(2):
        right = jnp.concatenate([pack[k, 1 + q] for pack in packs for k in range(2)], axis=0)
        acc[:, q * half : (q + 1) * half] = lax.dot_general(
            left, right, (((0,), (0,)), ((), ())), preferred_element_type=F32
        )
    for s in range(4):
        first = (at[2] + s) % 4
        for p in range(2):
            for q in range(4):
                row = jnp.where(
                    at[0] == 0,
                    p * 256 + first * 64 + q * 16,
                    q * 128 + p * 64 + first * 16,
                )
                k = (p * 4 + q) * 16
                outs[s][k : k + 16, :] = acc[pl.ds(pl.multiple_of(row, 16), 16), :]


def weight_part(at, packs):
    *_, samples, wide = packs[0].shape
    return pl.pallas_call(
        weight_kernel,
        in_specs=[SMEM] + [VMEM] * 4,
        out_specs=[VMEM] * 4,
        out_shape=[struct((wide // 4, 2 * wide), F32)] * 4,
        scratch_shapes=[pltpu.VMEM((wide, 2 * wide), F32)],
        compiler_params=params(24),
        cost_estimate=cost(4 * 10**10, 8 << 20),
    )(at, *packs)


def middle_kernel(*refs):
    parts, out = refs[:4], refs[4]
    acc = (parts[0][...] + parts[1][...]) + (parts[2][...] + parts[3][...])
    for k in range(8):
        out[k] = acc[k * 16 : (k + 1) * 16]


def middle(parts):
    rows, wide = parts[0].shape
    return pl.pallas_call(
        middle_kernel,
        in_specs=[VMEM] * 4,
        out_specs=VMEM,
        out_shape=struct((8, rows // 8, wide), F32),
        compiler_params=params(12),
        cost_estimate=cost(1 << 20, 3 << 20),
    )(*parts)


def last_kernel(parts, out):
    wide = parts.shape[2]
    for k in range(2):
        acc = (parts[4 * k] + parts[4 * k + 1]) + (parts[4 * k + 2] + parts[4 * k + 3])
        out[:, k * wide : (k + 1) * wide] = acc


def last(parts):
    _, rows, wide = parts.shape
    return pl.pallas_call(
        last_kernel,
        in_specs=[VMEM],
        out_specs=VMEM,
        out_shape=struct((rows, 2 * wide), F32),
        compiler_params=params(12),
        cost_estimate=cost(1 << 16, 1 << 18),
    )(parts)


def device(place):
    role, z, x, y = place
    return ((role * 4 + z) * 4 + x) * 4 + y


def along(value, axes, move):
    pairs = []
    for here in itertools.product(range(2), range(4), range(4), range(4)):
        to = list(here)
        axis = axes[here[0]]
        to[axis] = move(here[axis])
        pairs.append((device(here), device(to)))
    return lax.ppermute(value, AXES, pairs)


def around(values, axes):
    return [values[0]] + [
        along(value, axes, lambda i, s=s: (i + s) % 4) for s, value in enumerate(values) if s
    ]


def eights():
    groups = []
    for half, fixed in itertools.product(range(2), range(4)):
        both = [(2 * half + p, k) for p in range(2) for k in range(4)]
        groups.append([device((0, n, fixed, k)) for n, k in both])
        groups.append([device((1, k, n, fixed)) for n, k in both])
    return groups


def near_kernel(ids, near):
    bag_len, rows, slots = near.shape
    row = iota((rows, slots), 0)
    low, high = (row % 64).astype(F32), (row // 64).astype(F32)
    wanted = ids[...]
    wanted = jnp.where(wanted < 0, 4095, wanted)
    hi, lo = (wanted >> 6).astype(F32), (wanted & 63).astype(F32)
    for j in range(bag_len):
        part = jnp.where(lo[j : j + 1] == low, hi[j : j + 1] - high, -1.0)
        near[j] = part.astype(BF)


def nearby(ids):
    bag_len, slots = ids.shape
    return pl.pallas_call(
        near_kernel,
        in_specs=[VMEM],
        out_specs=VMEM,
        out_shape=struct((bag_len, 128, slots), BF),
        compiler_params=params(12),
        cost_estimate=cost(1 << 34, 1 << 20),
    )(ids)


def counts_kernel(near, after, out):
    block, slots = out.shape
    step = pl.program_id(0)
    one, zero = jnp.ones((), BF), jnp.zeros((), BF)
    for k in range(block // 128):
        chunk = step * (block // 128) + k
        here = jnp.full((128, slots), (2 * chunk).astype(F32), F32).astype(BF)
        count = jnp.where(near[0] == here, one, zero)
        for j in range(1, near.shape[0]):
            count = count + jnp.where(near[j] == here, one, zero)
        out[k * 128 : (k + 1) * 128, :] = count


def counts(near, rows, after):
    slots = near.shape[2]
    block = 512
    return pl.pallas_call(
        counts_kernel,
        grid=(rows // block,),
        in_specs=[pl.BlockSpec(near.shape, lambda i: (0, 0, 0)), HBM],
        out_specs=pl.BlockSpec((block, slots), lambda i: (i, 0)),
        out_shape=struct((rows, slots), BF),
        compiler_params=params(16),
        cost_estimate=cost(8 * rows * slots, 5 << 20),
    )(near, after)


def update_kernel(count, grads, table, accum, out):
    block, wide = table.shape
    step = pl.program_id(0)
    before = []
    for k in range(block // 128):
        chunk = step * (block // 128) + k
        before.append(jnp.broadcast_to(accum[pl.ds(chunk, 1), :], (128, 128)).T[:, 0:1])
    row_grad = dot(count[...], grads[...])
    square = jnp.sum(row_grad * row_grad, axis=1, keepdims=True)
    new_accum = jnp.concatenate(before, axis=0) + square * (1.0 / wide)
    out[...] = table[...] - row_grad * (learn_rate / jnp.sqrt(new_accum + 1e-6))


def update(count, grads, table, accum):
    rows, wide = table.shape
    slots = grads.shape[0]
    block = 256
    return pl.pallas_call(
        update_kernel,
        grid=(rows // block,),
        in_specs=[
            pl.BlockSpec((block, slots), lambda i: (i, 0)),
            pl.BlockSpec((slots, wide), lambda i: (0, 0)),
            pl.BlockSpec((block, wide), lambda i: (i, 0)),
            pl.BlockSpec(accum.shape, lambda i: (0, 0)),
        ],
        out_specs=pl.BlockSpec((block, wide), lambda i: (i, 0)),
        out_shape=struct((rows, wide), F32),
        compiler_params=params(58),
        cost_estimate=cost(4 * rows * slots * wide, 9 << 20),
    )(count, grads, table, accum)


def per_device(
    emb_table, row_accum, owners, local_rows, lengths, labels, w_hidden, hidden_bias, w_logit
):
    devices = lax.axis_size(AXES)
    samples, features, bag_len = local_rows.shape
    rows_dev, width = emb_table.shape
    cap = 2 * samples * features // devices
    role, z, x, y = (lax.axis_index(axis) for axis in AXES)
    odd = role == 1
    at = jnp.stack(
        [
            role,
            jnp.where(odd, x, z),
            jnp.where(odd, y, x),
        ]
    ).astype(I32)
    outgoing, cols, tgt_r = route(
        owners.transpose(1, 2, 0),
        local_rows.transpose(1, 2, 0),
        lengths.T,
        labels[None, :],
        devices,
        cap,
    )
    table_bf = emb_table.astype(BF)
    incoming = lax.all_to_all(outgoing, AXES, split_axis=0, concat_axis=0, tiled=True)
    found = lookup(incoming, table_bf, bag_len)
    slots = lax.all_to_all(
        found.reshape(devices, cap, width), AXES, split_axis=0, concat_axis=0, tiled=True
    ).reshape(devices * cap, width)
    ids_r = incoming.reshape(devices, bag_len, cap).transpose(1, 0, 2).reshape(bag_len, -1)
    near = nearby(ids_r)
    own, give, dpre = forward(
        at, slots, cols, hidden_bias[None, :], w_logit[None, :], w_hidden, features, near
    )
    got = lax.ppermute(give, "role", [(0, 1), (1, 0)])
    packs = merge(at, own, got)
    count = counts(near, rows_dev, packs[0])
    packs = around(packs, (1, 2))
    sending = backward(dpre, tgt_r, w_hidden, devices * cap, count)
    received = lax.all_to_all(
        sending.reshape(devices, cap, width), AXES, split_axis=0, concat_axis=0, tiled=True
    )
    new_table = update(
        count, received.reshape(devices * cap, width), emb_table, row_accum.reshape(-1, 128)
    )
    parts = around(weight_part(at, packs), (2, 3))
    *parts, new_table = lax.optimization_barrier((*parts, new_table))
    part = lax.all_to_all(
        middle(parts), AXES, split_axis=0, concat_axis=0, tiled=True, axis_index_groups=eights()
    )
    w_grad = last(part)
    return (new_table, w_grad)


def solution(mesh):
    split = Mesh(mesh.devices.reshape(2, 4, 4, 4), AXES)
    placed = (
        P(AXES, None),
        P(AXES),
        P(AXES, None, None),
        P(AXES, None, None),
        P(AXES, None),
        P(AXES),
        P(),
        P(),
        P(),
    )
    return jax.shard_map(
        per_device,
        mesh=split,
        in_specs=placed,
        out_specs=(P(AXES, None), P(AXES, None)),
        check_vma=False,
    )
```
